512 devices in a mesh: views: 4 (over x), depth: 32 (over y, z_hi), lat: 4 (over z_lo, core).
Axes of the slice: x: 4, y: 8, z: 8 (z_hi: 4, z_lo: 2; z = z_hi * 2 + z_lo), core: 2. Of those that a mesh axis runs over, the one named last changes fastest.
Arguments:
- density: bfloat16 [64, 2, 128, 2048], P(None, None, 'depth', 'lat'), may hold values from 0 to 3, as said below
- measured: float32 [16, 64, 2048], P('views', None, 'lat'), may hold values from 0 to 4
- shear_shift: int32 [16, 128], P('views', 'depth'), may hold values from -64 to 63
- shear_frac: float32 [16, 128], P('views', 'depth'), may hold values from 0 to 1
- spectrum: float32 [64], replicated, may hold values from 0.05 to 1
- attenuation: float32 [2, 64], replicated, may hold values from 0.3 to 6
Outputs:
- density_gradient: float32 [64, 2, 128, 2048], P('views', None, 'depth', 'lat')
The draws below stay inside these ranges and needn't reach their ends.
Inputs may be any that keep to these rules, and one draw needn't show every extreme that they name: `density`: densities are non-negative.
All inputs are finite; a program needn't handle non-finite values.
Results may differ from the reference program's by a relative error of at most 0.0016.
Values may be sent and summed in bfloat16 or wider, within the bound.
A program may use at most 64 MiB of HBM per device.

```python
import math
import jax
import jax.numpy as jnp
from jax import lax

M = 2
E = 64
Y = 64
HALO = 64
VIEWS = 16
Z = 128
X = 2048


def draw_density(key, part):
    key_cells, key_columns = jax.random.split(key)
    voxels = jax.random.uniform(key_cells, (Y, M, Z, X), jnp.float32, 0.0, 1.0)
    column_scale = jnp.exp(jax.random.uniform(key_columns, (Y, M, 1, X), jnp.float32, math.log(0.2), math.log(2.0)))
    return (voxels * column_scale).astype(jnp.bfloat16)


def with_ends(array, key, low, high):
    extent = array.shape
    place = [jax.random.randint(jax.random.fold_in(key, axis), (), 0, extent[axis]) for axis in range(len(extent))]
    array = array.at[tuple(place)].set(low)
    longest = extent.index(max(extent))
    place[longest] = (place[longest] + 1) % extent[longest]
    return array.at[tuple(place)].set(high)


def level_of(own_key, dims, cuts, low, largest):
    factor_of = 1.0
    for position, parts in cuts:
        draws = jax.random.uniform(jax.random.fold_in(jax.random.fold_in(own_key, 6), position), (parts,), jnp.float32, low / len(cuts), largest / len(cuts))
        factor_of = factor_of * jnp.repeat(jnp.exp(draws), dims[position] // parts).reshape((-1,) + (1,) * (len(dims) - 1 - position))
    return factor_of


def setup_inputs(seed: int = 0) -> dict:
    key_of = jax.random.split(jax.random.key(seed), 7)
    density = draw_density(jax.random.fold_in(key_of[6], 71), 0)
    measured = jnp.clip(4.0 * jax.random.uniform(key_of[1], (VIEWS, Y, X), jnp.float32) ** level_of(key_of[1], (VIEWS, Y, X), ((0, 4), (2, 4)), -0.2, 0.2), 0.0, 4.0)
    shear_shift = with_ends(jax.random.randint(key_of[2], (VIEWS, Z), 0 - HALO, HALO), jax.random.fold_in(key_of[2], 1), 0 - HALO, HALO - 1).astype(jnp.int32)
    shear_frac = jnp.clip(1.0 * jax.random.uniform(key_of[3], (VIEWS, Z), jnp.float32) ** level_of(key_of[3], (VIEWS, Z), ((0, 4), (1, 32)), -0.2, 0.2), 0.0, 1.0)
    spectrum = jnp.clip(jnp.exp(jax.random.uniform(key_of[4], (E,), jnp.float32, math.log(0.05), math.log(1.0))), 0.05, 1.0)
    attenuation = jnp.clip(jnp.exp(jax.random.uniform(key_of[5], (M, E), jnp.float32, math.log(0.3), math.log(6.0))), 0.3, 6.0)
    return {"density": density, "measured": measured, "shear_shift": shear_shift, "shear_frac": shear_frac, "spectrum": spectrum, "attenuation": attenuation}


def spectral_grad(path_water, path_bone, observed, spectrum, attenuation, views_all):
    coefficients = jnp.concatenate([jnp.ones((1, spectrum.shape[0]), jnp.float32), attenuation], axis=0)
    exponent = attenuation[0][:, None, None] * path_water[None] + attenuation[1][:, None, None] * path_bone[None]
    counts = spectrum[:, None, None] * jnp.exp(-exponent)
    moments = jnp.einsum('ke,eyx->kyx', coefficients, counts, precision=lax.Precision.HIGHEST)
    intensity = moments[0]
    residual = jnp.log(jnp.sum(spectrum)) - jnp.log(intensity) - observed
    factor = residual / intensity / views_all
    return (moments[1:] * factor[None]).astype(jnp.bfloat16)

def reference(density, measured, shear_shift, shear_frac, spectrum, attenuation):
    views_all = measured.shape[0]
    row_total, materials, depth_all, width_all = density.shape
    lower_weight = lax.optimization_barrier((1.0 - shear_frac).astype(jnp.bfloat16)).astype(jnp.float32)
    upper_weight = lax.optimization_barrier(shear_frac.astype(jnp.bfloat16)).astype(jnp.float32)
    padded = jnp.pad(density, ((0, 0), (0, 0), (0, 0), (HALO, HALO)))
    positions = jnp.arange(depth_all, dtype=jnp.int32)

    def forward_step(running, depth_pos):
        slab_plane = lax.dynamic_index_in_dim(padded, depth_pos, 2, keepdims=False).astype(jnp.float32)

        def one_view(offset, lower_tap_weight, upper_tap_weight):
            lower_tap = lax.dynamic_slice_in_dim(slab_plane, offset + HALO, width_all, 2)
            upper_tap = lax.dynamic_slice_in_dim(slab_plane, offset + HALO + 1, width_all, 2)
            return lower_tap_weight * lower_tap + upper_tap_weight * upper_tap
        sheared = jax.vmap(one_view)(shear_shift[:, depth_pos], lower_weight[:, depth_pos], upper_weight[:, depth_pos])
        return (running + sheared, None)
    initial = jnp.zeros((views_all, row_total, materials, width_all), jnp.float32)
    path_sums, _ = lax.scan(forward_step, initial, positions)
    path_sums = path_sums / depth_all

    def per_view(inputs):
        return spectral_grad(inputs[0], inputs[1], inputs[2], spectrum, attenuation, views_all)
    path_grads = lax.map(per_view, (path_sums[:, :, 0, :], path_sums[:, :, 1, :], measured))
    path_grads = lax.optimization_barrier(jnp.transpose(path_grads, (0, 2, 1, 3)))
    padded_grads = jnp.pad(path_grads, ((0, 0), (0, 0), (0, 0), (HALO, HALO))).astype(jnp.float32)

    def back_step(carry, depth_pos):

        def one_view(grid, offset, lower_tap_weight, upper_tap_weight):
            lower_tap = lax.dynamic_slice_in_dim(grid, HALO - offset, width_all, 2)
            upper_tap = lax.dynamic_slice_in_dim(grid, HALO - offset - 1, width_all, 2)
            return lower_tap_weight * lower_tap + upper_tap_weight * upper_tap
        layer = lax.optimization_barrier(jnp.sum(jax.vmap(one_view)(padded_grads, shear_shift[:, depth_pos], lower_weight[:, depth_pos], upper_weight[:, depth_pos]), axis=0))
        return (carry, layer)
    _, layers = lax.scan(back_step, jnp.zeros((), jnp.float32), positions)
    return jnp.transpose(layers, (1, 2, 0, 3))
```

```python
import functools

import jax
import jax.numpy as jnp
from jax import lax
from jax.experimental import pallas as pl
from jax.experimental.pallas import tpu as pltpu
from jax.sharding import PartitionSpec as P

HALO = 64
LANES = 128
MESH = pl.DeviceIdType.MESH
(SHX_SEND, SHX_RECV, SH_SEND, SH_RECV, OWN_SEND, LEFT_SEND, RIGHT_SEND, ROWS_LOCAL, ROWS_SEND,
 ROWS_RECV, EDGE_SEND, EDGE_RECV, OUT_SEND, OUT_RECV) = range(14)


def take_lanes(x, index):
    return jnp.take_along_axis(x, index, axis=1, mode="promise_in_bounds")


def kernel(
    sizes, dens, meas, shift, frac, spec, att, out, slabs, planes, rows_in, rows_mine, rows_all,
    shear_x, shear_mine, shear_all, shear_pair, shift_wide, weight_wide, acc, low_rows, up_rows,
    grads, product, sems, own_recv, halo_recv,
):
    group_count, depth_count, lat_count = sizes
    views_here, depth_here, materials = shift.shape[0], shift.shape[1], dens.shape[1]
    rows_here = depth_count // 2
    view_count = group_count * views_here
    pair_count = depth_count // 2
    batches = own_recv.shape[0]
    batch = depth_count // batches
    pairs = batch // 2
    bins = spec.shape[0]
    group = lax.axis_index("views")
    depth = lax.axis_index("depth")
    lat = lax.axis_index("lat")
    half = depth % 2
    has_left = lat > 0
    has_right = lat < lat_count - 1
    halo_from = jnp.where(half == 0, lat - 1, lat + 1)
    has_halo = jnp.where(half == 0, lat, lat_count - 1 - lat) > 0
    halo_to = jnp.where(half == 0, lat + 1, lat - 1)
    gives_halo = jnp.where(half == 0, lat_count - 1 - lat, lat) > 0

    def at(group_to, depth_to, lat_to):
        return {"views": group_to, "depth": depth_to, "lat": lat_to}

    def remote(src, dst, send, recv, to):
        return pltpu.make_async_remote_copy(
            src_ref=src, dst_ref=dst, send_sem=send, recv_sem=recv, device_id=to, device_id_type=MESH
        )

    def drain(ref, sem):
        pltpu.make_async_copy(ref, ref, sem).wait()

    def lanes(start, width):
        return pl.ds(pl.multiple_of(start, LANES), width)

    tile_row = pl.multiple_of((depth // 2) // 8 * 8, 8) if rows_here >= 8 else 0
    tile_rows = rows_in.shape[2]
    row_loads = [
        pltpu.make_async_copy(
            meas.at[:, pl.ds(pl.multiple_of(g * rows_here + tile_row, tile_rows), tile_rows), :],
            rows_in.at[g],
            sems.at[ROWS_LOCAL],
        )
        for g in range(group_count)
    ]
    for load in row_loads:
        load.start()

    barrier = pltpu.get_barrier_semaphore()

    def greet(to):
        pl.semaphore_signal(barrier, inc=1, device_id=to, device_id_type=MESH)

    def greet_depth(k, carry):
        greet(at(group, (depth + k) % depth_count, lat))
        return carry

    lax.fori_loop(1, depth_count, greet_depth, 0)
    for g in range(1, group_count):
        greet(at((group + g) % group_count, depth, lat))

    @pl.when(has_halo)
    def _():
        def greet_halo(k, carry):
            greet(at(group, (depth + k) % depth_count, halo_from))
            return carry

        lax.fori_loop(0, depth_count, greet_halo, 0)
        for g in range(1, group_count):
            greet(at((group + g) % group_count, depth, halo_from))

    sub = lax.broadcasted_iota(jnp.int32, (depth_here, LANES), 0)
    lane4 = lax.broadcasted_iota(jnp.int32, (depth_here, LANES), 1)
    place = lane4 % 32 - group * views_here
    shifts = jnp.zeros((depth_here, LANES), jnp.int32)
    fracs = jnp.zeros((depth_here, LANES), jnp.float32)
    for v in range(views_here):
        for z in range(depth_here):
            here = (sub == z) & (place == v)
            shifts = jnp.where(here, shift[v, z] + HALO, shifts)
            fracs = jnp.where(here, frac[v, z], fracs)
    mine = (place >= 0) & (place < views_here) & (lane4 < 96)
    weights = jnp.where(lane4 < 64, 1.0 - fracs, fracs).astype(jnp.bfloat16).astype(jnp.float32)
    shear_x[group] = jnp.where(mine, jnp.where(lane4 < 32, shifts.astype(jnp.float32), weights), 0.0)

    @pl.when(jnp.logical_not(has_halo) & (half == 0))
    def _():
        slabs[:, :, :, 0:LANES] = jnp.zeros((depth_count, materials, depth_here, LANES), jnp.bfloat16)

    @pl.when(jnp.logical_not(has_halo) & (half == 1))
    def _():
        slabs[:, :, :, 3 * LANES : 4 * LANES] = jnp.zeros(
            (depth_count, materials, depth_here, LANES), jnp.bfloat16
        )

    some = (depth_count + 1) // 2
    expected = (
        depth_count - 1 + group_count - 1
        + jnp.where(has_left, depth_count // 2, 0)
        + jnp.where(has_right, depth_count // 2, 0)
        + jnp.where(gives_halo, group_count - 1, 0)
    )
    pl.semaphore_wait(barrier, expected)

    for g in range(1, group_count):
        remote(
            shear_x.at[group], shear_x.at[group], sems.at[SHX_SEND], sems.at[SHX_RECV],
            at((group + g) % group_count, depth, lat),
        ).start()

    mine_batch = depth // batch

    def own_part(depth_to):
        half_to = depth_to % 2
        src = dens.at[group * rows_here + depth_to // 2, :, :, lanes(half_to * LANES, 3 * LANES)]
        dst = slabs.at[depth, :, :, lanes((1 - half_to) * LANES, 3 * LANES)]
        return src, dst

    def send_own(k, carry):
        depth_to = (depth + k) % depth_count
        src, dst = own_part(depth_to)
        remote(
            src, dst, sems.at[OWN_SEND], own_recv.at[mine_batch], at(group, depth_to, lat)
        ).start()
        return carry

    src, dst = own_part(depth)
    pltpu.make_async_copy(src, dst, own_recv.at[mine_batch]).start()
    lax.fori_loop(1, some, send_own, 0)

    drain(shear_x.at[0 : group_count - 1], sems.at[SHX_RECV])
    table = shear_x[0]
    for g in range(1, group_count):
        table = table + shear_x[g]
    shear_mine[...] = table
    shear_all[depth] = table

    def send_shear(k, carry):
        depth_to = (depth + k) % depth_count
        remote(
            shear_mine, shear_all.at[depth], sems.at[SH_SEND], sems.at[SH_RECV], at(group, depth_to, lat)
        ).start()
        return carry

    lax.fori_loop(1, depth_count, send_shear, 0)
    lax.fori_loop(some, depth_count, send_own, 0)

    @pl.when(has_right)
    def _():
        def send_right(k, carry):
            depth_to = 2 * ((depth // 2 + k) % pair_count)
            remote(
                dens.at[group * rows_here + depth_to // 2, :, :, 3 * LANES : 4 * LANES],
                slabs.at[depth, :, :, 0:LANES],
                sems.at[RIGHT_SEND], halo_recv.at[mine_batch], at(group, depth_to, lat + 1),
            ).start()
            return carry

        lax.fori_loop(0, pair_count, send_right, 0)

    @pl.when(has_left)
    def _():
        def send_left(k, carry):
            depth_to = 2 * ((depth // 2 + k) % pair_count) + 1
            remote(
                dens.at[group * rows_here + depth_to // 2, :, :, 0:LANES],
                slabs.at[depth, :, :, 3 * LANES : 4 * LANES],
                sems.at[LEFT_SEND], halo_recv.at[mine_batch], at(group, depth_to, lat - 1),
            ).start()
            return carry

        lax.fori_loop(0, pair_count, send_left, 0)

    drain(rows_in, sems.at[ROWS_LOCAL])
    row = (depth // 2) % tile_rows
    for g in range(group_count):
        for v in range(views_here):
            rows_mine[g, v : v + 1, :] = rows_in[g, v, pl.ds(row, 1), :]
    for k in range(group_count):
        g = (group + k) % group_count
        src = rows_mine.at[g, :, lanes(half * LANES, 3 * LANES)]
        dst = rows_all.at[group, :, lanes((1 - half) * LANES, 3 * LANES)]
        if k == 0:
            pltpu.make_async_copy(src, dst, sems.at[ROWS_RECV]).start()
        else:
            remote(src, dst, sems.at[ROWS_SEND], sems.at[ROWS_RECV], at(g, depth, lat)).start()

    @pl.when(gives_halo)
    def _():
        for k in range(group_count):
            g = (group + k) % group_count
            remote(
                rows_mine.at[g, :, lanes((1 - half) * (3 * LANES), LANES)],
                rows_all.at[group, :, lanes(half * (3 * LANES), LANES)],
                sems.at[EDGE_SEND], sems.at[EDGE_RECV], at(g, depth, halo_to),
            ).start()

    lane = lax.broadcasted_iota(jnp.int32, (8, LANES), 1)
    drain(shear_all.at[0 : depth_count - 1], sems.at[SH_RECV])

    def join_shear(p, carry):
        shear_pair[p] = jnp.concatenate([shear_all[2 * p], shear_all[2 * p + 1]], axis=0)
        return carry

    lax.fori_loop(0, pair_count, join_shear, 0)

    for t in range(batches):
        b = (mine_batch + t) % batches
        drain(slabs.at[pl.ds(b * batch, batch), :, :, 0 : 3 * LANES], own_recv.at[b])

        @pl.when(has_halo)
        def _():
            drain(slabs.at[pl.ds(b * batch, batch), :, :, 0:LANES], halo_recv.at[b])

        for p in range(pairs):
            for m in range(materials):
                first = slabs[b * batch + 2 * p, m].astype(jnp.float32)
                second = slabs[b * batch + 2 * p + 1, m].astype(jnp.float32)
                planes[p, m] = jnp.concatenate([first, second], axis=0)

        def one_view(v, carry):
            zero = jnp.zeros((8, LANES), jnp.float32)
            low = [[zero if t == 0 else acc[v, m, k] for k in range(3)] for m in range(materials)]
            up = [[zero if t == 0 else acc[v, m, 3 + k] for k in range(4)] for m in range(materials)]
            for p in range(pairs):
                pair = b * pairs + p
                shear = shear_pair[pair]
                pick = jnp.full((8, LANES), v, jnp.int32)
                start = take_lanes(shear, pick).astype(jnp.int32)
                lower = take_lanes(shear, pick + 32)
                upper = take_lanes(shear, pick + 64)
                shift_wide[v, pair] = start
                weight_wide[v, pair, 0] = lower
                weight_wide[v, pair, 1] = upper
                moved = lane + start
                index = moved & (LANES - 1)
                inside = moved < LANES
                for m in range(materials):
                    parts = [
                        take_lanes(planes[p, m, :, k * LANES : (k + 1) * LANES], index) for k in range(4)
                    ]
                    for k in range(3):
                        tap = jnp.where(inside, parts[k], parts[k + 1])
                        low[m][k] = low[m][k] + lower * tap
                        up[m][k] = up[m][k] + upper * tap
                    up[m][3] = up[m][3] + upper * parts[3]
            for m in range(materials):
                for k in range(3):
                    acc[v, m, k] = low[m][k]
                for k in range(4):
                    acc[v, m, 3 + k] = up[m][k]
            return carry

        lax.fori_loop(0, view_count, one_view, 0)

    for v in range(view_count):
        for m in range(materials):
            for k in range(3):
                low_rows[m, v : v + 1, k * LANES : (k + 1) * LANES] = jnp.sum(
                    acc[v, m, k], axis=0, keepdims=True
                )
            for k in range(4):
                up_rows[m, v : v + 1, k * LANES : (k + 1) * LANES] = jnp.sum(
                    acc[v, m, 3 + k], axis=0, keepdims=True
                )
    depth_all = depth_here * depth_count
    paths = [
        (low_rows[m] + pltpu.roll(up_rows[m], 4 * LANES - 1, 1)[:, 0 : 3 * LANES]) * (1.0 / depth_all)
        for m in range(materials)
    ]

    drain(rows_all.at[:, :, 0 : 3 * LANES], sems.at[ROWS_RECV])

    @pl.when(has_halo)
    def _():
        drain(rows_all.at[:, :, 0:LANES], sems.at[EDGE_RECV])

    observed = jnp.concatenate([rows_all[g] for g in range(group_count)], axis=0)
    observed = pltpu.roll(observed, 4 * LANES - HALO, 1)[:, 0 : 3 * LANES]
    blank = jnp.zeros((view_count, 3 * LANES), jnp.float32)

    def one_bin(e, carry):
        intensity, water, bone, total = carry
        counts = spec[e] * jnp.exp(-(att[0, e] * paths[0] + att[1, e] * paths[1]))
        return (
            intensity + counts, water + att[0, e] * counts, bone + att[1, e] * counts, total + spec[e]
        )

    intensity, water, bone, total = lax.fori_loop(
        0, bins, one_bin, (blank, blank, blank, jnp.float32(0.0)), unroll=4
    )
    residual = jnp.log(blank + total) - jnp.log(intensity) - observed
    factor = residual / intensity / view_count
    column = lax.broadcasted_iota(jnp.int32, (view_count, 3 * LANES), 1)
    column = column + (lat * 4 + half * 2) * LANES - HALO
    valid = (column >= 0) & (column < lat_count * 4 * LANES)
    for m, moment in enumerate((water, bone)):
        gradient = jnp.where(valid, (moment * factor).astype(jnp.bfloat16).astype(jnp.float32), 0.0)
        for v in range(view_count):
            for k in range(3):
                grads[m, v, k] = jnp.broadcast_to(
                    gradient[v : v + 1, k * LANES : (k + 1) * LANES], (8, LANES)
                )

    part = pl.ds(pl.multiple_of(half * (2 * LANES), LANES), 2 * LANES)

    def one_pair(t, carry):
        pair = (depth // 2 + 1 + t) % pair_count
        zero = jnp.zeros((8, LANES), jnp.float32)

        def add_view(v, sums):
            moved = lane + (LANES - 1) - shift_wide[v, pair]
            index = moved & (LANES - 1)
            inside = moved < LANES
            lower = weight_wide[v, pair, 0]
            upper = weight_wide[v, pair, 1]
            result = []
            for m in range(materials):
                a0, a1, a2, b0, b1 = sums[m]
                parts = [take_lanes(grads[m, v, k], index) for k in range(3)]
                tap0 = jnp.where(inside, parts[0], parts[1])
                tap1 = jnp.where(inside, parts[1], parts[2])
                result.append((
                    a0 + lower * tap0, a1 + lower * tap1, a2 + lower * parts[2],
                    b0 + upper * tap0, b1 + upper * tap1,
                ))
            return tuple(result)

        sums = lax.fori_loop(0, view_count, add_view, ((zero,) * 5,) * materials, unroll=4)
        for m in range(materials):
            a0, a1, a2, b0, b1 = sums[m]
            ahead = pltpu.roll(jnp.concatenate([a0, a1, a2], axis=1), 3 * LANES - 1, 1)[:, 0 : 2 * LANES]
            result = ahead + jnp.concatenate([b0, b1], axis=1)
            product[2 * pair, m] = result[0:depth_here]
            product[2 * pair + 1, m] = result[depth_here : 2 * depth_here]
        for side in range(2):
            depth_to = 2 * pair + side
            src, dst = product.at[depth_to], out.at[depth // 2, :, :, part]

            @pl.when(depth_to != depth)
            def _():
                remote(src, dst, sems.at[OUT_SEND], sems.at[OUT_RECV], at(group, depth_to, lat)).start()

            @pl.when(depth_to == depth)
            def _():
                pltpu.make_async_copy(src, dst, sems.at[OUT_RECV]).start()

        return carry

    lax.fori_loop(0, pair_count, one_pair, 0)

    others = depth_count - 1
    drain(shear_x.at[0 : group_count - 1], sems.at[SHX_SEND])
    drain(shear_all.at[0:others], sems.at[SH_SEND])
    drain(slabs.at[0:others, :, :, 0 : 3 * LANES], sems.at[OWN_SEND])
    drain(rows_all.at[0 : group_count - 1, :, 0 : 3 * LANES], sems.at[ROWS_SEND])

    @pl.when(has_right)
    def _():
        drain(slabs.at[0:pair_count, :, :, 0:LANES], sems.at[RIGHT_SEND])

    @pl.when(has_left)
    def _():
        drain(slabs.at[0:pair_count, :, :, 0:LANES], sems.at[LEFT_SEND])

    @pl.when(gives_halo)
    def _():
        drain(rows_all.at[:, :, 0:LANES], sems.at[EDGE_SEND])

    drain(product.at[0:others], sems.at[OUT_SEND])
    drain(out, sems.at[OUT_RECV])


def per_device(density, measured, shear_shift, shear_frac, spectrum, attenuation):
    sizes = tuple(lax.axis_size(name) for name in ("views", "depth", "lat"))
    group_count, depth_count, lat_count = sizes
    row_total, materials, depth_here, tile_width = density.shape
    views_here = shear_shift.shape[0]
    view_count = views_here * group_count
    rows_out = row_total // group_count
    pair_count = depth_count // 2
    batch = min(8, depth_count)
    batches = depth_count // batch
    tile_rows = min(8, rows_out)
    f32, bf16 = jnp.float32, jnp.bfloat16
    anywhere = pl.BlockSpec(memory_space=pl.ANY)
    scalars = pl.BlockSpec(memory_space=pltpu.SMEM)
    return pl.pallas_call(
        functools.partial(kernel, sizes),
        out_shape=jax.ShapeDtypeStruct((rows_out, materials, depth_here, tile_width), f32),
        in_specs=[anywhere, anywhere, scalars, scalars, scalars, scalars],
        out_specs=anywhere,
        scratch_shapes=[
            pltpu.VMEM((depth_count, materials, depth_here, tile_width), bf16),
            pltpu.VMEM((batch // 2, materials, 8, tile_width), f32),
            pltpu.VMEM((group_count, views_here, tile_rows, tile_width), f32),
            pltpu.VMEM((group_count, views_here, tile_width), f32),
            pltpu.VMEM((group_count, views_here, tile_width), f32),
            pltpu.VMEM((group_count, depth_here, LANES), f32),
            pltpu.VMEM((depth_here, LANES), f32),
            pltpu.VMEM((depth_count, depth_here, LANES), f32),
            pltpu.VMEM((pair_count, 8, LANES), f32),
            pltpu.VMEM((view_count, pair_count, 8, LANES), jnp.int32),
            pltpu.VMEM((view_count, pair_count, 2, 8, LANES), f32),
            pltpu.VMEM((view_count, materials, 7, 8, LANES), f32),
            pltpu.VMEM((materials, view_count, 3 * LANES), f32),
            pltpu.VMEM((materials, view_count, 4 * LANES), f32),
            pltpu.VMEM((materials, view_count, 3, 8, LANES), f32),
            pltpu.VMEM((depth_count, materials, depth_here, 2 * LANES), f32),
            pltpu.SemaphoreType.DMA((14,)),
            pltpu.SemaphoreType.DMA((batches,)),
            pltpu.SemaphoreType.DMA((batches,)),
        ],
        compiler_params=pltpu.CompilerParams(
            collective_id=0, has_side_effects=True, vmem_limit_bytes=32 * 2**20
        ),
        cost_estimate=pl.CostEstimate(
            flops=16 * 2**20, bytes_accessed=2 * 2**20, transcendentals=2**19
        ),
    )(density, measured, shear_shift, shear_frac, spectrum, attenuation)


def solution(mesh):
    in_specs = (
        P(None, None, "depth", "lat"),
        P("views", None, "lat"),
        P("views", "depth"),
        P("views", "depth"),
        P(),
        P(),
    )
    out_specs = P("views", None, "depth", "lat")
    return jax.shard_map(
        per_device, mesh=mesh, in_specs=in_specs, out_specs=out_specs, check_vma=False
    )
```

```python
import functools

import jax
import jax.numpy as jnp
from jax import lax
from jax.experimental import pallas as pl
from jax.experimental.pallas import tpu as pltpu
from jax.sharding import PartitionSpec as P

HALO = 64
LANES = 128
MESH = pl.DeviceIdType.MESH
KINDS = 3 * LANES
(SHX_SEND, SHX_RECV, SH_SEND, SH_RECV, OWN_SEND, LEFT_SEND, RIGHT_SEND, ROWS_LOCAL, ROWS_SEND,
 ROWS_RECV, EDGE_SEND, EDGE_RECV, OUT_SEND, OUT_RECV, OWN_RECV, HALO_RECV) = range(16)


def take_lanes(x, index):
    return jnp.take_along_axis(x, index, axis=1, mode="promise_in_bounds")


def kernel(
    sizes, dens, meas, shift_in, frac_in, spec_in, att_in, out, shift, frac, spec, att, slabs, planes, rows_in, rows_mine, rows_all,
    shear_x, shear_mine, shear_all, spread, shift_wide, weight_wide, acc, low_rows, up_rows,
    grads, product, sems, small_sems,
):
    group_count, depth_count, lat_count = sizes
    views_here, depth_here, materials = shift.shape[0], shift.shape[1], dens.shape[1]
    rows_here = depth_count // 2
    view_count = group_count * views_here
    pair_count = depth_count // 2
    z_count = 4
    y_count = depth_count // z_count
    bins = spec.shape[0]
    group = lax.axis_index("views")
    depth = lax.axis_index("depth")
    lat = lax.axis_index("lat")
    half = depth % 2
    has_left = lat > 0
    has_right = lat < lat_count - 1
    halo_from = jnp.where(half == 0, lat - 1, lat + 1)
    has_halo = jnp.where(half == 0, lat, lat_count - 1 - lat) > 0
    halo_to = jnp.where(half == 0, lat + 1, lat - 1)
    gives_halo = jnp.where(half == 0, lat_count - 1 - lat, lat) > 0

    def at(group_to, depth_to, lat_to):
        return {"views": group_to, "depth": depth_to, "lat": lat_to}

    def remote(src, dst, send, recv, to):
        return pltpu.make_async_remote_copy(
            src_ref=src, dst_ref=dst, send_sem=send, recv_sem=recv, device_id=to, device_id_type=MESH
        )

    def far_first(step, count):
        return count // 2 + jnp.where(step % 2 == 1, -((step + 1) // 2), step // 2)

    def partner(step):
        y_to = (depth // z_count + far_first(step // z_count, y_count)) % y_count
        z_to = (depth % z_count + far_first(step % z_count, z_count)) % z_count
        return y_to * z_count + z_to

    def drain(ref, sem):
        pltpu.make_async_copy(ref, ref, sem).wait()

    def lanes(start, width):
        return pl.ds(pl.multiple_of(start, LANES), width)

    tile_row = pl.multiple_of((depth // 2) // 8 * 8, 8) if rows_here >= 8 else 0
    tile_rows = rows_in.shape[2]
    row_loads = [
        pltpu.make_async_copy(
            meas.at[:, pl.ds(pl.multiple_of(g * rows_here + tile_row, tile_rows), tile_rows), :],
            rows_in.at[g],
            sems.at[ROWS_LOCAL],
        )
        for g in range(group_count)
    ]
    small_loads = [
        pltpu.make_async_copy(src, dst, small_sems.at[k])
        for k, (src, dst) in enumerate(((shift_in, shift), (frac_in, frac), (spec_in, spec), (att_in, att)))
    ]
    for load in small_loads + row_loads:
        load.start()

    barrier = pltpu.get_barrier_semaphore()

    def greet(to):
        pl.semaphore_signal(barrier, inc=1, device_id=to, device_id_type=MESH)

    def greet_depth(k, carry):
        greet(at(group, (depth + k) % depth_count, lat))
        return carry

    lax.fori_loop(1, depth_count, greet_depth, 0)
    for g in range(1, group_count):
        greet(at((group + g) % group_count, depth, lat))

    @pl.when(has_halo)
    def _():
        def greet_halo(k, carry):
            greet(at(group, (depth + k) % depth_count, halo_from))
            return carry

        lax.fori_loop(0, depth_count, greet_halo, 0)
        for g in range(1, group_count):
            greet(at((group + g) % group_count, depth, halo_from))

    sub = lax.broadcasted_iota(jnp.int32, (depth_here, LANES), 0)
    lane4 = lax.broadcasted_iota(jnp.int32, (depth_here, LANES), 1)
    place = lane4 % 32 - group * views_here
    for load in small_loads[:2]:
        load.wait()
    shifts = jnp.zeros((depth_here, LANES), jnp.int32)
    fracs = jnp.zeros((depth_here, LANES), jnp.float32)
    for v in range(views_here):
        for z in range(depth_here):
            here = (sub == z) & (place == v)
            shifts = jnp.where(here, shift[v, z] + HALO, shifts)
            fracs = jnp.where(here, frac[v, z], fracs)
    mine = (place >= 0) & (place < views_here) & (lane4 < 96)
    weights = jnp.where(lane4 < 64, 1.0 - fracs, fracs).astype(jnp.bfloat16).astype(jnp.float32)
    shear_x[group] = jnp.where(mine, jnp.where(lane4 < 32, shifts.astype(jnp.float32), weights), 0.0)

    some = depth_count // 2
    expected = (
        depth_count - 1 + group_count - 1
        + jnp.where(has_left, depth_count // 2, 0)
        + jnp.where(has_right, depth_count // 2, 0)
        + jnp.where(gives_halo, group_count - 1, 0)
    )
    pl.semaphore_wait(barrier, expected)

    for g in range(1, group_count):
        remote(
            shear_x.at[group], shear_x.at[group], sems.at[SHX_SEND], sems.at[SHX_RECV],
            at((group + g) % group_count, depth, lat),
        ).start()

    def own_part(depth_to):
        half_to = depth_to % 2
        src = dens.at[group * rows_here + depth_to // 2, :, :, lanes(half_to * LANES, 3 * LANES)]
        dst = slabs.at[depth, :, :, lanes((1 - half_to) * LANES, 3 * LANES)]
        return src, dst

    def send_halo(depth_to):
        here = dens.at[group * rows_here + depth_to // 2]

        @pl.when((depth_to % 2 == 0) & has_right)
        def _():
            remote(
                here.at[:, :, 3 * LANES : 4 * LANES], slabs.at[depth, :, :, 0:LANES],
                sems.at[RIGHT_SEND], sems.at[HALO_RECV], at(group, depth_to, lat + 1),
            ).start()

        @pl.when((depth_to % 2 == 1) & has_left)
        def _():
            remote(
                here.at[:, :, 0:LANES], slabs.at[depth, :, :, 3 * LANES : 4 * LANES],
                sems.at[LEFT_SEND], sems.at[HALO_RECV], at(group, depth_to, lat - 1),
            ).start()

    def send_slab(k, carry):
        depth_to = partner(k)
        src, dst = own_part(depth_to)
        remote(
            src, dst, sems.at[OWN_SEND], sems.at[OWN_RECV], at(group, depth_to, lat)
        ).start()
        send_halo(depth_to)
        return carry

    src, dst = own_part(depth)
    pltpu.make_async_copy(src, dst, sems.at[OWN_RECV]).start()
    lax.fori_loop(0, some, send_slab, 0)

    drain(shear_x.at[0 : group_count - 1], sems.at[SHX_RECV])
    table = shear_x[0]
    for g in range(1, group_count):
        table = table + shear_x[g]
    shear_mine[...] = table
    shear_all[depth] = table

    def send_shear(k, carry):
        depth_to = partner(k)
        remote(
            shear_mine, shear_all.at[depth], sems.at[SH_SEND], sems.at[SH_RECV], at(group, depth_to, lat)
        ).start()
        return carry

    lax.fori_loop(0, depth_count - 1, send_shear, 0)
    lax.fori_loop(some, depth_count - 1, send_slab, 0)
    send_halo(depth)

    @pl.when(jnp.logical_not(has_halo) & (half == 0))
    def _():
        slabs[:, :, :, 0:LANES] = jnp.zeros((depth_count, materials, depth_here, LANES), jnp.bfloat16)

    @pl.when(jnp.logical_not(has_halo) & (half == 1))
    def _():
        slabs[:, :, :, 3 * LANES : 4 * LANES] = jnp.zeros(
            (depth_count, materials, depth_here, LANES), jnp.bfloat16
        )

    drain(rows_in, sems.at[ROWS_LOCAL])
    row = (depth // 2) % tile_rows
    for g in range(group_count):
        for v in range(views_here):
            rows_mine[g, v : v + 1, :] = rows_in[g, v, pl.ds(row, 1), :]
    for k in range(group_count):
        g = (group + k) % group_count
        src = rows_mine.at[g, :, lanes(half * LANES, 3 * LANES)]
        dst = rows_all.at[group, :, lanes((1 - half) * LANES, 3 * LANES)]
        if k == 0:
            pltpu.make_async_copy(src, dst, sems.at[ROWS_RECV]).start()
        else:
            remote(src, dst, sems.at[ROWS_SEND], sems.at[ROWS_RECV], at(g, depth, lat)).start()

    @pl.when(gives_halo)
    def _():
        for k in range(group_count):
            g = (group + k) % group_count
            remote(
                rows_mine.at[g, :, lanes((1 - half) * (3 * LANES), LANES)],
                rows_all.at[group, :, lanes(half * (3 * LANES), LANES)],
                sems.at[EDGE_SEND], sems.at[EDGE_RECV], at(g, depth, halo_to),
            ).start()

    source = lax.broadcasted_iota(jnp.int32, (LANES, KINDS), 0)
    wanted = lax.broadcasted_iota(jnp.int32, (LANES, KINDS), 1) // LANES * 32
    for v in range(view_count):
        spread[v] = (source == wanted + v).astype(jnp.float32).astype(jnp.bfloat16)

    lane = lax.broadcasted_iota(jnp.int32, (8, LANES), 1)
    drain(shear_all.at[0 : depth_count - 1], sems.at[SH_RECV])
    table = jnp.concatenate([shear_all[p] for p in range(depth_count)], axis=0).astype(jnp.bfloat16)

    def widen(v, carry):
        wide = jnp.dot(table, spread[v], preferred_element_type=jnp.float32)
        for p in range(pair_count):
            rows = wide[8 * p : 8 * p + 8]
            shift_wide[v, p] = rows[:, 0:LANES].astype(jnp.int32)
            weight_wide[v, p, 0] = rows[:, LANES : 2 * LANES]
            weight_wide[v, p, 1] = rows[:, 2 * LANES : 3 * LANES]
        return carry

    lax.fori_loop(0, view_count, widen, 0, unroll=4)

    drain(slabs.at[:, :, :, 0 : 3 * LANES], sems.at[OWN_RECV])

    @pl.when(has_halo)
    def _():
        drain(slabs.at[:, :, :, 0:LANES], sems.at[HALO_RECV])

    for p in range(pair_count):
        for m in range(materials):
            first = slabs[2 * p, m].astype(jnp.float32)
            second = slabs[2 * p + 1, m].astype(jnp.float32)
            planes[p, m] = jnp.concatenate([first, second], axis=0)

    def one_view(v, carry):
        zero = jnp.zeros((8, LANES), jnp.float32)
        low = [[zero] * 3 for m in range(materials)]
        up = [[zero] * 4 for m in range(materials)]
        for pair in range(pair_count):
            moved = lane + shift_wide[v, pair]
            index = moved & (LANES - 1)
            inside = moved < LANES
            lower = weight_wide[v, pair, 0]
            upper = weight_wide[v, pair, 1]
            for m in range(materials):
                parts = [
                    take_lanes(planes[pair, m, :, k * LANES : (k + 1) * LANES], index) for k in range(4)
                ]
                for k in range(3):
                    tap = jnp.where(inside, parts[k], parts[k + 1])
                    low[m][k] = low[m][k] + lower * tap
                    up[m][k] = up[m][k] + upper * tap
                up[m][3] = up[m][3] + upper * parts[3]
        for m in range(materials):
            for k in range(3):
                acc[v, m, k] = low[m][k]
            for k in range(4):
                acc[v, m, 3 + k] = up[m][k]
        return carry

    lax.fori_loop(0, view_count, one_view, 0)

    for v in range(view_count):
        for m in range(materials):
            for k in range(3):
                low_rows[m, v : v + 1, k * LANES : (k + 1) * LANES] = jnp.sum(
                    acc[v, m, k], axis=0, keepdims=True
                )
            for k in range(4):
                up_rows[m, v : v + 1, k * LANES : (k + 1) * LANES] = jnp.sum(
                    acc[v, m, 3 + k], axis=0, keepdims=True
                )
    depth_all = depth_here * depth_count
    paths = [
        (low_rows[m] + pltpu.roll(up_rows[m], 4 * LANES - 1, 1)[:, 0 : 3 * LANES]) * (1.0 / depth_all)
        for m in range(materials)
    ]

    drain(rows_all.at[:, :, 0 : 3 * LANES], sems.at[ROWS_RECV])

    @pl.when(has_halo)
    def _():
        drain(rows_all.at[:, :, 0:LANES], sems.at[EDGE_RECV])

    observed = jnp.concatenate([rows_all[g] for g in range(group_count)], axis=0)
    observed = pltpu.roll(observed, 4 * LANES - HALO, 1)[:, 0 : 3 * LANES]
    blank = jnp.zeros((view_count, 3 * LANES), jnp.float32)
    for load in small_loads[2:]:
        load.wait()

    def one_bin(e, carry):
        intensity, water, bone, total = carry
        counts = spec[e] * jnp.exp(-(att[0, e] * paths[0] + att[1, e] * paths[1]))
        return (
            intensity + counts, water + att[0, e] * counts, bone + att[1, e] * counts, total + spec[e]
        )

    intensity, water, bone, total = lax.fori_loop(
        0, bins, one_bin, (blank, blank, blank, jnp.float32(0.0)), unroll=4
    )
    residual = jnp.log(blank + total) - jnp.log(intensity) - observed
    factor = residual / intensity / view_count
    column = lax.broadcasted_iota(jnp.int32, (view_count, 3 * LANES), 1)
    column = column + (lat * 4 + half * 2) * LANES - HALO
    valid = (column >= 0) & (column < lat_count * 4 * LANES)
    for m, moment in enumerate((water, bone)):
        grads[m] = jnp.where(valid, (moment * factor).astype(jnp.bfloat16).astype(jnp.float32), 0.0)

    part = pl.ds(pl.multiple_of(half * (2 * LANES), LANES), 2 * LANES)

    def one_pair(t, carry):
        y_to = (depth // z_count + far_first(t // 2, y_count)) % y_count
        pair = y_to * 2 + (depth % z_count // 2 + 1 + t) % 2
        zero = jnp.zeros((8, LANES), jnp.float32)
        sums = [(zero,) * 5 for m in range(materials)]
        for v in range(view_count):
            moved = lane + (LANES - 1) - shift_wide[v, pair]
            index = moved & (LANES - 1)
            inside = moved < LANES
            lower = weight_wide[v, pair, 0]
            upper = weight_wide[v, pair, 1]
            for m in range(materials):
                a0, a1, a2, b0, b1 = sums[m]
                parts = [
                    take_lanes(
                        jnp.broadcast_to(grads[m, v : v + 1, k * LANES : (k + 1) * LANES], (8, LANES)), index
                    )
                    for k in range(3)
                ]
                tap0 = jnp.where(inside, parts[0], parts[1])
                tap1 = jnp.where(inside, parts[1], parts[2])
                sums[m] = (
                    a0 + lower * tap0, a1 + lower * tap1, a2 + lower * parts[2],
                    b0 + upper * tap0, b1 + upper * tap1,
                )
        for m in range(materials):
            a0, a1, a2, b0, b1 = sums[m]
            ahead = pltpu.roll(jnp.concatenate([a0, a1, a2], axis=1), 3 * LANES - 1, 1)[:, 0 : 2 * LANES]
            result = ahead + jnp.concatenate([b0, b1], axis=1)
            product[2 * pair, m] = result[0:depth_here]
            product[2 * pair + 1, m] = result[depth_here : 2 * depth_here]
        for side in range(2):
            depth_to = 2 * pair + side
            src, dst = product.at[depth_to], out.at[depth // 2, :, :, part]

            @pl.when(depth_to != depth)
            def _():
                remote(src, dst, sems.at[OUT_SEND], sems.at[OUT_RECV], at(group, depth_to, lat)).start()

            @pl.when(depth_to == depth)
            def _():
                pltpu.make_async_copy(src, dst, sems.at[OUT_RECV]).start()

        return carry

    lax.fori_loop(0, pair_count, one_pair, 0)

    others = depth_count - 1
    drain(shear_x.at[0 : group_count - 1], sems.at[SHX_SEND])
    drain(shear_all.at[0:others], sems.at[SH_SEND])
    drain(slabs.at[0:others, :, :, 0 : 3 * LANES], sems.at[OWN_SEND])
    drain(rows_all.at[0 : group_count - 1, :, 0 : 3 * LANES], sems.at[ROWS_SEND])

    @pl.when(has_right)
    def _():
        drain(slabs.at[0:pair_count, :, :, 0:LANES], sems.at[RIGHT_SEND])

    @pl.when(has_left)
    def _():
        drain(slabs.at[0:pair_count, :, :, 0:LANES], sems.at[LEFT_SEND])

    @pl.when(gives_halo)
    def _():
        drain(rows_all.at[:, :, 0:LANES], sems.at[EDGE_SEND])

    drain(product.at[0:others], sems.at[OUT_SEND])
    drain(out, sems.at[OUT_RECV])


def per_device(density, measured, shear_shift, shear_frac, spectrum, attenuation):
    sizes = tuple(lax.axis_size(name) for name in ("views", "depth", "lat"))
    group_count, depth_count, lat_count = sizes
    row_total, materials, depth_here, tile_width = density.shape
    views_here = shear_shift.shape[0]
    view_count = views_here * group_count
    rows_out = row_total // group_count
    pair_count = depth_count // 2
    tile_rows = min(8, rows_out)
    f32, bf16 = jnp.float32, jnp.bfloat16
    hbm = pl.BlockSpec(memory_space=pltpu.HBM)
    return pl.pallas_call(
        functools.partial(kernel, sizes),
        out_shape=jax.ShapeDtypeStruct((rows_out, materials, depth_here, tile_width), f32),
        in_specs=[hbm] * 6,
        out_specs=pl.BlockSpec(memory_space=pl.ANY),
        scratch_shapes=[
            pltpu.SMEM(shear_shift.shape, jnp.int32),
            pltpu.SMEM(shear_frac.shape, f32),
            pltpu.SMEM(spectrum.shape, f32),
            pltpu.SMEM(attenuation.shape, f32),
            pltpu.VMEM((depth_count, materials, depth_here, tile_width), bf16),
            pltpu.VMEM((pair_count, materials, 8, tile_width), f32),
            pltpu.VMEM((group_count, views_here, tile_rows, tile_width), f32),
            pltpu.VMEM((group_count, views_here, tile_width), f32),
            pltpu.VMEM((group_count, views_here, tile_width), f32),
            pltpu.VMEM((group_count, depth_here, LANES), f32),
            pltpu.VMEM((depth_here, LANES), f32),
            pltpu.VMEM((depth_count, depth_here, LANES), f32),
            pltpu.VMEM((view_count, LANES, KINDS), bf16),
            pltpu.VMEM((view_count, pair_count, 8, LANES), jnp.int32),
            pltpu.VMEM((view_count, pair_count, 2, 8, LANES), f32),
            pltpu.VMEM((view_count, materials, 7, 8, LANES), f32),
            pltpu.VMEM((materials, view_count, 3 * LANES), f32),
            pltpu.VMEM((materials, view_count, 4 * LANES), f32),
            pltpu.VMEM((materials, view_count, 3 * LANES), f32),
            pltpu.VMEM((depth_count, materials, depth_here, 2 * LANES), f32),
            pltpu.SemaphoreType.DMA((16,)),
            pltpu.SemaphoreType.DMA((4,)),
        ],
        compiler_params=pltpu.CompilerParams(
            collective_id=0, has_side_effects=True, vmem_limit_bytes=60 * 2**20
        ),
        cost_estimate=pl.CostEstimate(
            flops=16 * 2**20, bytes_accessed=2 * 2**20, transcendentals=2**19
        ),
    )(density, measured, shear_shift, shear_frac, spectrum, attenuation)


def solution(mesh):
    in_specs = (
        P(None, None, "depth", "lat"),
        P("views", None, "lat"),
        P("views", "depth"),
        P("views", "depth"),
        P(),
        P(),
    )
    out_specs = P("views", None, "depth", "lat")
    return jax.shard_map(
        per_device, mesh=mesh, in_specs=in_specs, out_specs=out_specs, check_vma=False
    )
```

```python
import functools
import math

import jax
import jax.numpy as jnp
from jax import lax
from jax.experimental import pallas as pl
from jax.experimental.pallas import tpu as pltpu
from jax.sharding import PartitionSpec as P

HALO = 64
LANES = 128
MESH = pl.DeviceIdType.MESH
FLOOR = 2.0**-17
STEPS = 32767.0 / math.log(1.0 + 256.0 / FLOOR)
KINDS = 3 * LANES
(SHX_SEND, SHX_RECV, SH_SEND, SH_RECV, OWN_SEND, LEFT_SEND, RIGHT_SEND, ROWS_LOCAL, ROWS_SEND,
 ROWS_RECV, EDGE_SEND, EDGE_RECV, OUT_SEND, OUT_RECV) = range(14)


def take_lanes(x, index):
    return jnp.take_along_axis(x, index, axis=1, mode="promise_in_bounds")


def encode(x):
    size = jnp.log(1.0 + jnp.abs(x) * (1.0 / FLOOR)) * STEPS
    return jnp.round(jnp.where(x < 0.0, -size, size)).astype(jnp.int32).astype(jnp.int16)


def decode(code):
    code = code.astype(jnp.float32)
    size = (jnp.exp(jnp.abs(code) * (1.0 / STEPS)) - 1.0) * FLOOR
    return jnp.where(code < 0.0, -size, size)


def kernel(
    sizes, dens, meas, shift_in, frac_in, spec_in, att_in, out, shift, frac, spec, att, slabs, planes, rows_in, rows_mine, rows_all,
    shear_x, shear_mine, shear_all, spread, shift_wide, weight_wide, acc, low_rows, up_rows,
    grads, product, sems, own_recv, halo_recv, small_sems,
):
    group_count, depth_count, lat_count = sizes
    views_here, depth_here, materials = shift.shape[0], shift.shape[1], dens.shape[1]
    rows_here = depth_count // 2
    view_count = group_count * views_here
    pair_count = depth_count // 2
    z_count = 4
    y_count = depth_count // z_count
    first_part = 1 + 2 * (y_count // 4) if y_count % 2 == 0 else y_count
    parts_of = [(0, first_part), (first_part, y_count)] if first_part < y_count else [(0, y_count)]
    batches = len(parts_of)
    split = first_part * z_count
    bins = spec.shape[0]
    group = lax.axis_index("views")
    depth = lax.axis_index("depth")
    lat = lax.axis_index("lat")
    half = depth % 2
    y_here, z_here = lax.div(depth, z_count), lax.rem(depth, z_count)
    has_left = lat > 0
    has_right = lat < lat_count - 1
    halo_from = jnp.where(half == 0, lat - 1, lat + 1)
    has_halo = jnp.where(half == 0, lat, lat_count - 1 - lat) > 0
    halo_to = jnp.where(half == 0, lat + 1, lat - 1)
    gives_halo = jnp.where(half == 0, lat_count - 1 - lat, lat) > 0

    def at(group_to, depth_to, lat_to):
        return {"views": group_to, "depth": depth_to, "lat": lat_to}

    def remote(src, dst, send, recv, to):
        return pltpu.make_async_remote_copy(
            src_ref=src, dst_ref=dst, send_sem=send, recv_sem=recv, device_id=to, device_id_type=MESH
        )

    def far_first(step, count):
        if isinstance(step, int):
            return count // 2 + (-((step + 1) // 2) if step % 2 else step // 2)
        return count // 2 + jnp.where(step % 2 == 1, -((step + 1) // 2), step // 2)

    def partner(step):
        y_step = far_first(step // z_count, y_count)
        z_step = far_first(step % z_count, z_count)
        y_to = lax.rem(y_here + jnp.where(lat % 2 == 1, y_count - y_step, y_step), y_count)
        z_to = lax.rem(z_here + jnp.where(lat % 2 == 1, z_count - z_step, z_step), z_count)
        return y_to * z_count + z_to

    def drain(ref, sem):
        pltpu.make_async_copy(ref, ref, sem).wait()

    def lanes(start, width):
        return pl.ds(pl.multiple_of(start, LANES), width)

    tile_row = pl.multiple_of((depth // 2) // 8 * 8, 8) if rows_here >= 8 else 0
    tile_rows = rows_in.shape[2]
    row_loads = [
        pltpu.make_async_copy(
            meas.at[:, pl.ds(pl.multiple_of(g * rows_here + tile_row, tile_rows), tile_rows), :],
            rows_in.at[g],
            sems.at[ROWS_LOCAL],
        )
        for g in range(group_count)
    ]
    small_loads = [
        pltpu.make_async_copy(src, dst, small_sems.at[k])
        for k, (src, dst) in enumerate(((shift_in, shift), (frac_in, frac), (spec_in, spec), (att_in, att)))
    ]
    for load in small_loads + row_loads:
        load.start()

    barrier = pltpu.get_barrier_semaphore()

    def greet(to):
        pl.semaphore_signal(barrier, inc=1, device_id=to, device_id_type=MESH)

    def greet_depth(k, carry):
        greet(at(group, (depth + k) % depth_count, lat))
        return carry

    lax.fori_loop(1, depth_count, greet_depth, 0)
    for g in range(1, group_count):
        greet(at((group + g) % group_count, depth, lat))

    @pl.when(has_halo)
    def _():
        def greet_halo(k, carry):
            greet(at(group, (depth + k) % depth_count, halo_from))
            return carry

        lax.fori_loop(0, depth_count, greet_halo, 0)
        for g in range(1, group_count):
            greet(at((group + g) % group_count, depth, halo_from))

    sub = lax.broadcasted_iota(jnp.int32, (depth_here, LANES), 0)
    lane4 = lax.broadcasted_iota(jnp.int32, (depth_here, LANES), 1)
    place = lane4 % 32 - group * views_here
    for load in small_loads[:2]:
        load.wait()
    shifts = jnp.zeros((depth_here, LANES), jnp.int32)
    fracs = jnp.zeros((depth_here, LANES), jnp.float32)
    for v in range(views_here):
        for z in range(depth_here):
            here = (sub == z) & (place == v)
            shifts = jnp.where(here, shift[v, z] + HALO, shifts)
            fracs = jnp.where(here, frac[v, z], fracs)
    mine = (place >= 0) & (place < views_here) & (lane4 < 96)
    weights = jnp.where(lane4 < 64, 1.0 - fracs, fracs).astype(jnp.bfloat16).astype(jnp.float32)
    shear_x[group] = jnp.where(mine, jnp.where(lane4 < 32, shifts.astype(jnp.float32), weights), 0.0)

    some = min(depth_count // 2, split)
    expected = (
        depth_count - 1 + group_count - 1
        + jnp.where(has_left, depth_count // 2, 0)
        + jnp.where(has_right, depth_count // 2, 0)
        + jnp.where(gives_halo, group_count - 1, 0)
    )
    pl.semaphore_wait(barrier, expected)

    for g in range(1, group_count):
        remote(
            shear_x.at[group], shear_x.at[group], sems.at[SHX_SEND], sems.at[SHX_RECV],
            at((group + g) % group_count, depth, lat),
        ).start()

    def own_part(depth_to):
        half_to = depth_to % 2
        src = dens.at[group * rows_here + depth_to // 2, :, :, lanes(half_to * LANES, 3 * LANES)]
        dst = slabs.at[depth, :, :, lanes((1 - half_to) * LANES, 3 * LANES)]
        return src, dst

    def send_halo(depth_to, batch):
        here = dens.at[group * rows_here + depth_to // 2]

        @pl.when((depth_to % 2 == 0) & has_right)
        def _():
            remote(
                here.at[:, :, 3 * LANES : 4 * LANES], slabs.at[depth, :, :, 0:LANES],
                sems.at[RIGHT_SEND], halo_recv.at[batch], at(group, depth_to, lat + 1),
            ).start()

        @pl.when((depth_to % 2 == 1) & has_left)
        def _():
            remote(
                here.at[:, :, 0:LANES], slabs.at[depth, :, :, 3 * LANES : 4 * LANES],
                sems.at[LEFT_SEND], halo_recv.at[batch], at(group, depth_to, lat - 1),
            ).start()

    def send_slab(batch, k, carry):
        depth_to = partner(k)
        src, dst = own_part(depth_to)
        remote(
            src, dst, sems.at[OWN_SEND], own_recv.at[batch], at(group, depth_to, lat)
        ).start()
        send_halo(depth_to, batch)
        return carry

    src, dst = own_part(depth)
    pltpu.make_async_copy(src, dst, own_recv.at[batches - 1]).start()
    lax.fori_loop(0, some, functools.partial(send_slab, 0), 0)

    drain(shear_x.at[0 : group_count - 1], sems.at[SHX_RECV])
    table = shear_x[0]
    for g in range(1, group_count):
        table = table + shear_x[g]
    shear_mine[...] = table
    shear_all[depth] = table

    def send_shear(k, carry):
        depth_to = partner(k)
        remote(
            shear_mine, shear_all.at[depth], sems.at[SH_SEND], sems.at[SH_RECV], at(group, depth_to, lat)
        ).start()
        return carry

    lax.fori_loop(0, depth_count - 1, send_shear, 0)
    lax.fori_loop(some, min(split, depth_count - 1), functools.partial(send_slab, 0), 0)
    lax.fori_loop(split, depth_count - 1, functools.partial(send_slab, batches - 1), 0)
    send_halo(depth, batches - 1)

    @pl.when(jnp.logical_not(has_halo) & (half == 0))
    def _():
        slabs[:, :, :, 0:LANES] = jnp.zeros((depth_count, materials, depth_here, LANES), jnp.bfloat16)

    @pl.when(jnp.logical_not(has_halo) & (half == 1))
    def _():
        slabs[:, :, :, 3 * LANES : 4 * LANES] = jnp.zeros(
            (depth_count, materials, depth_here, LANES), jnp.bfloat16
        )

    drain(rows_in, sems.at[ROWS_LOCAL])
    row = (depth // 2) % tile_rows
    for g in range(group_count):
        for v in range(views_here):
            rows_mine[g, v : v + 1, :] = rows_in[g, v, pl.ds(row, 1), :]
    for k in range(group_count):
        g = (group + k) % group_count
        src = rows_mine.at[g, :, lanes(half * LANES, 3 * LANES)]
        dst = rows_all.at[group, :, lanes((1 - half) * LANES, 3 * LANES)]
        if k == 0:
            pltpu.make_async_copy(src, dst, sems.at[ROWS_RECV]).start()
        else:
            remote(src, dst, sems.at[ROWS_SEND], sems.at[ROWS_RECV], at(g, depth, lat)).start()

    @pl.when(gives_halo)
    def _():
        for k in range(group_count):
            g = (group + k) % group_count
            remote(
                rows_mine.at[g, :, lanes((1 - half) * (3 * LANES), LANES)],
                rows_all.at[group, :, lanes(half * (3 * LANES), LANES)],
                sems.at[EDGE_SEND], sems.at[EDGE_RECV], at(g, depth, halo_to),
            ).start()

    source = lax.broadcasted_iota(jnp.int32, (LANES, KINDS), 0)
    wanted = lax.broadcasted_iota(jnp.int32, (LANES, KINDS), 1) // LANES * 32
    for v in range(view_count):
        spread[v] = (source == wanted + v).astype(jnp.float32).astype(jnp.bfloat16)

    lane = lax.broadcasted_iota(jnp.int32, (8, LANES), 1)
    drain(shear_all.at[0 : depth_count - 1], sems.at[SH_RECV])
    table = jnp.concatenate([shear_all[p] for p in range(depth_count)], axis=0).astype(jnp.bfloat16)

    def widen(v, carry):
        wide = jnp.dot(table, spread[v], preferred_element_type=jnp.float32)
        for p in range(pair_count):
            rows = wide[8 * p : 8 * p + 8]
            shift_wide[v, p] = rows[:, 0:LANES].astype(jnp.int32)
            weight_wide[v, p, 0] = rows[:, LANES : 2 * LANES]
            weight_wide[v, p, 1] = rows[:, 2 * LANES : 3 * LANES]
        return carry

    lax.fori_loop(0, view_count, widen, 0, unroll=4)

    for batch, (step_from, step_to) in enumerate(parts_of):
        share = (step_to - step_from) * z_count
        drain(slabs.at[0:share, :, :, 0 : 3 * LANES], own_recv.at[batch])

        @pl.when(has_halo)
        def _():
            drain(slabs.at[0:share, :, :, 0:LANES], halo_recv.at[batch])

        pairs = []
        for step in range(step_from, step_to):
            y_step = far_first(step, y_count)
            y_from = lax.rem(y_here + jnp.where(lat % 2 == 1, y_step, y_count - y_step), y_count)
            pairs += [2 * y_from, 2 * y_from + 1]
        for p, pair in enumerate(pairs):
            for m in range(materials):
                first = slabs[2 * pair, m].astype(jnp.float32)
                second = slabs[2 * pair + 1, m].astype(jnp.float32)
                planes[p, m] = jnp.concatenate([first, second], axis=0)

        def one_view(v, carry):
            zero = jnp.zeros((8, LANES), jnp.float32)
            low = [[zero if batch == 0 else acc[v, m, k] for k in range(3)] for m in range(materials)]
            up = [[zero if batch == 0 else acc[v, m, 3 + k] for k in range(4)] for m in range(materials)]
            for p, pair in enumerate(pairs):
                moved = lane + shift_wide[v, pair]
                index = moved & (LANES - 1)
                inside = moved < LANES
                lower = weight_wide[v, pair, 0]
                upper = weight_wide[v, pair, 1]
                for m in range(materials):
                    parts = [
                        take_lanes(planes[p, m, :, k * LANES : (k + 1) * LANES], index) for k in range(4)
                    ]
                    for k in range(3):
                        tap = jnp.where(inside, parts[k], parts[k + 1])
                        low[m][k] = low[m][k] + lower * tap
                        up[m][k] = up[m][k] + upper * tap
                    up[m][3] = up[m][3] + upper * parts[3]
            for m in range(materials):
                for k in range(3):
                    acc[v, m, k] = low[m][k]
                for k in range(4):
                    acc[v, m, 3 + k] = up[m][k]
            return carry

        lax.fori_loop(0, view_count, one_view, 0, unroll=4)

    for v in range(view_count):
        for m in range(materials):
            for k in range(3):
                low_rows[m, v : v + 1, k * LANES : (k + 1) * LANES] = jnp.sum(
                    acc[v, m, k], axis=0, keepdims=True
                )
            for k in range(4):
                up_rows[m, v : v + 1, k * LANES : (k + 1) * LANES] = jnp.sum(
                    acc[v, m, 3 + k], axis=0, keepdims=True
                )
    depth_all = depth_here * depth_count
    paths = [
        (low_rows[m] + pltpu.roll(up_rows[m], 4 * LANES - 1, 1)[:, 0 : 3 * LANES]) * (1.0 / depth_all)
        for m in range(materials)
    ]

    drain(rows_all.at[:, :, 0 : 3 * LANES], sems.at[ROWS_RECV])

    @pl.when(has_halo)
    def _():
        drain(rows_all.at[:, :, 0:LANES], sems.at[EDGE_RECV])

    observed = jnp.concatenate([rows_all[g] for g in range(group_count)], axis=0)
    observed = pltpu.roll(observed, 4 * LANES - HALO, 1)[:, 0 : 3 * LANES]
    blank = jnp.zeros((view_count, 3 * LANES), jnp.float32)
    for load in small_loads[2:]:
        load.wait()

    def one_bin(e, carry):
        intensity, water, bone, total = carry
        counts = spec[e] * jnp.exp(-(att[0, e] * paths[0] + att[1, e] * paths[1]))
        return (
            intensity + counts, water + att[0, e] * counts, bone + att[1, e] * counts, total + spec[e]
        )

    intensity, water, bone, total = lax.fori_loop(
        0, bins, one_bin, (blank, blank, blank, jnp.float32(0.0)), unroll=4
    )
    residual = jnp.log(blank + total) - jnp.log(intensity) - observed
    factor = residual / intensity / view_count
    column = lax.broadcasted_iota(jnp.int32, (view_count, 3 * LANES), 1)
    column = column + (lat * 4 + half * 2) * LANES - HALO
    valid = (column >= 0) & (column < lat_count * 4 * LANES)
    for m, moment in enumerate((water, bone)):
        grads[m] = jnp.where(valid, (moment * factor).astype(jnp.bfloat16).astype(jnp.float32), 0.0)

    part = pl.ds(pl.multiple_of(half * (2 * LANES), LANES), 2 * LANES)

    def one_pair(t, carry):
        y_step = far_first(t // 2, y_count)
        y_to = lax.rem(y_here + jnp.where(lat % 2 == 1, y_count - y_step, y_step), y_count)
        pair = y_to * 2 + (depth % z_count // 2 + 1 + t) % 2
        zero = jnp.zeros((8, LANES), jnp.float32)
        sums = [(zero,) * 5 for m in range(materials)]
        for v in range(view_count):
            moved = lane + (LANES - 1) - shift_wide[v, pair]
            index = moved & (LANES - 1)
            inside = moved < LANES
            lower = weight_wide[v, pair, 0]
            upper = weight_wide[v, pair, 1]
            for m in range(materials):
                a0, a1, a2, b0, b1 = sums[m]
                parts = [
                    take_lanes(
                        jnp.broadcast_to(grads[m, v : v + 1, k * LANES : (k + 1) * LANES], (8, LANES)), index
                    )
                    for k in range(3)
                ]
                tap0 = jnp.where(inside, parts[0], parts[1])
                tap1 = jnp.where(inside, parts[1], parts[2])
                sums[m] = (
                    a0 + lower * tap0, a1 + lower * tap1, a2 + lower * parts[2],
                    b0 + upper * tap0, b1 + upper * tap1,
                )
        for m in range(materials):
            a0, a1, a2, b0, b1 = sums[m]
            ahead = pltpu.roll(jnp.concatenate([a0, a1, a2], axis=1), 3 * LANES - 1, 1)[:, 0 : 2 * LANES]
            result = encode(ahead + jnp.concatenate([b0, b1], axis=1))
            product[2 * pair, m] = result[0:depth_here]
            product[2 * pair + 1, m] = result[depth_here : 2 * depth_here]
        for side in range(2):
            depth_to = 2 * pair + side
            src, dst = product.at[depth_to], out.at[depth // 2, :, :, part]

            @pl.when(depth_to != depth)
            def _():
                remote(src, dst, sems.at[OUT_SEND], sems.at[OUT_RECV], at(group, depth_to, lat)).start()

            @pl.when(depth_to == depth)
            def _():
                pltpu.make_async_copy(src, dst, sems.at[OUT_RECV]).start()

        return carry

    lax.fori_loop(0, pair_count, one_pair, 0, unroll=2)

    others = depth_count - 1
    drain(shear_x.at[0 : group_count - 1], sems.at[SHX_SEND])
    drain(shear_all.at[0:others], sems.at[SH_SEND])
    drain(slabs.at[0:others, :, :, 0 : 3 * LANES], sems.at[OWN_SEND])
    drain(rows_all.at[0 : group_count - 1, :, 0 : 3 * LANES], sems.at[ROWS_SEND])

    @pl.when(has_right)
    def _():
        drain(slabs.at[0:pair_count, :, :, 0:LANES], sems.at[RIGHT_SEND])

    @pl.when(has_left)
    def _():
        drain(slabs.at[0:pair_count, :, :, 0:LANES], sems.at[LEFT_SEND])

    @pl.when(gives_halo)
    def _():
        drain(rows_all.at[:, :, 0:LANES], sems.at[EDGE_SEND])

    drain(product.at[0:others], sems.at[OUT_SEND])
    drain(out, sems.at[OUT_RECV])


def per_device(density, measured, shear_shift, shear_frac, spectrum, attenuation):
    sizes = tuple(lax.axis_size(name) for name in ("views", "depth", "lat"))
    group_count, depth_count, lat_count = sizes
    row_total, materials, depth_here, tile_width = density.shape
    views_here = shear_shift.shape[0]
    view_count = views_here * group_count
    rows_out = row_total // group_count
    pair_count = depth_count // 2
    tile_rows = min(8, rows_out)
    f32, bf16 = jnp.float32, jnp.bfloat16
    hbm = pl.BlockSpec(memory_space=pltpu.HBM)
    codes = pl.pallas_call(
        functools.partial(kernel, sizes),
        out_shape=jax.ShapeDtypeStruct((rows_out, materials, depth_here, tile_width), jnp.int16),
        in_specs=[hbm] * 6,
        out_specs=pl.BlockSpec(memory_space=pl.ANY),
        scratch_shapes=[
            pltpu.SMEM(shear_shift.shape, jnp.int32),
            pltpu.SMEM(shear_frac.shape, f32),
            pltpu.SMEM(spectrum.shape, f32),
            pltpu.SMEM(attenuation.shape, f32),
            pltpu.VMEM((depth_count, materials, depth_here, tile_width), bf16),
            pltpu.VMEM((pair_count, materials, 8, tile_width), f32),
            pltpu.VMEM((group_count, views_here, tile_rows, tile_width), f32),
            pltpu.VMEM((group_count, views_here, tile_width), f32),
            pltpu.VMEM((group_count, views_here, tile_width), f32),
            pltpu.VMEM((group_count, depth_here, LANES), f32),
            pltpu.VMEM((depth_here, LANES), f32),
            pltpu.VMEM((depth_count, depth_here, LANES), f32),
            pltpu.VMEM((view_count, LANES, KINDS), bf16),
            pltpu.VMEM((view_count, pair_count, 8, LANES), jnp.int32),
            pltpu.VMEM((view_count, pair_count, 2, 8, LANES), f32),
            pltpu.VMEM((view_count, materials, 7, 8, LANES), f32),
            pltpu.VMEM((materials, view_count, 3 * LANES), f32),
            pltpu.VMEM((materials, view_count, 4 * LANES), f32),
            pltpu.VMEM((materials, view_count, 3 * LANES), f32),
            pltpu.VMEM((depth_count, materials, depth_here, 2 * LANES), jnp.int16),
            pltpu.SemaphoreType.DMA((14,)),
            pltpu.SemaphoreType.DMA((2,)),
            pltpu.SemaphoreType.DMA((2,)),
            pltpu.SemaphoreType.DMA((4,)),
        ],
        compiler_params=pltpu.CompilerParams(
            collective_id=0, has_side_effects=True, vmem_limit_bytes=60 * 2**20
        ),
        cost_estimate=pl.CostEstimate(
            flops=16 * 2**20, bytes_accessed=2 * 2**20, transcendentals=2**19
        ),
    )(density, measured, shear_shift, shear_frac, spectrum, attenuation)
    return decode(codes)


def solution(mesh):
    in_specs = (
        P(None, None, "depth", "lat"),
        P("views", None, "lat"),
        P("views", "depth"),
        P("views", "depth"),
        P(),
        P(),
    )
    out_specs = P("views", None, "depth", "lat")
    return jax.shard_map(
        per_device, mesh=mesh, in_specs=in_specs, out_specs=out_specs, check_vma=False
    )
```

```python
import functools
import math

import jax
import jax.numpy as jnp
from jax import lax
from jax.experimental import pallas as pl
from jax.experimental.pallas import tpu as pltpu
from jax.sharding import PartitionSpec as P

HALO = 64
LANES = 128
MESH = pl.DeviceIdType.MESH
FLOOR = 2.0**-17
STEPS = 32767.0 / math.log(1.0 + 256.0 / FLOOR)
KINDS = 3 * LANES
(SHX_SEND, SHX_RECV, SH_SEND, SH_RECV, OWN_SEND, LEFT_SEND, RIGHT_SEND, ROWS_LOCAL, ROWS_SEND,
 ROWS_RECV, EDGE_SEND, EDGE_RECV, OUT_SEND, OUT_RECV) = range(14)


def take_lanes(x, index):
    return jnp.take_along_axis(x, index, axis=1, mode="promise_in_bounds")


def encode(x):
    size = jnp.log(1.0 + jnp.abs(x) * (1.0 / FLOOR)) * STEPS
    return jnp.round(jnp.where(x < 0.0, -size, size)).astype(jnp.int32).astype(jnp.int16)


def decode(code):
    code = code.astype(jnp.float32)
    size = (jnp.exp(jnp.abs(code) * (1.0 / STEPS)) - 1.0) * FLOOR
    return jnp.where(code < 0.0, -size, size)


def kernel(
    sizes, dens, meas, shift_in, frac_in, spec_in, att_in, out, shift, frac, spec, att, held, slabs, planes, rows_in, rows_mine, rows_all,
    shear_x, shear_mine, shear_all, spread, shift_wide, weight_wide, acc, low_rows, up_rows,
    grads, product, sems, own_recv, halo_recv, small_sems,
):
    group_count, depth_count, lat_count = sizes
    views_here, depth_here, materials = shift.shape[0], shift.shape[1], dens.shape[1]
    rows_here = depth_count // 2
    view_count = group_count * views_here
    pair_count = depth_count // 2
    z_count = 4
    y_count = depth_count // z_count
    first_part = 1 + 2 * (y_count // 4) if y_count % 2 == 0 else y_count
    parts_of = [(0, first_part), (first_part, y_count)] if first_part < y_count else [(0, y_count)]
    batches = len(parts_of)
    split = first_part * z_count
    bins = spec.shape[0]
    group = lax.axis_index("views")
    depth = lax.axis_index("depth")
    lat = lax.axis_index("lat")
    half = depth % 2
    y_here, z_here = lax.div(depth, z_count), lax.rem(depth, z_count)
    has_left = lat > 0
    has_right = lat < lat_count - 1
    halo_from = jnp.where(half == 0, lat - 1, lat + 1)
    has_halo = jnp.where(half == 0, lat, lat_count - 1 - lat) > 0
    halo_to = jnp.where(half == 0, lat + 1, lat - 1)
    gives_halo = jnp.where(half == 0, lat_count - 1 - lat, lat) > 0

    def at(group_to, depth_to, lat_to):
        return {"views": group_to, "depth": depth_to, "lat": lat_to}

    def remote(src, dst, send, recv, to):
        return pltpu.make_async_remote_copy(
            src_ref=src, dst_ref=dst, send_sem=send, recv_sem=recv, device_id=to, device_id_type=MESH
        )

    def far_first(step, count):
        if isinstance(step, int):
            return count // 2 + (-((step + 1) // 2) if step % 2 else step // 2)
        return count // 2 + jnp.where(step % 2 == 1, -((step + 1) // 2), step // 2)

    def partner(step):
        y_step = far_first(step // z_count, y_count)
        z_step = far_first(step % z_count, z_count)
        y_to = lax.rem(y_here + jnp.where(lat % 2 == 1, y_count - y_step, y_step), y_count)
        z_to = lax.rem(z_here + jnp.where(lat % 2 == 1, z_count - z_step, z_step), z_count)
        return y_to * z_count + z_to

    def drain(ref, sem):
        pltpu.make_async_copy(ref, ref, sem).wait()

    def lanes(start, width):
        return pl.ds(pl.multiple_of(start, LANES), width)

    tile_row = pl.multiple_of((depth // 2) // 8 * 8, 8) if rows_here >= 8 else 0
    tile_rows = rows_in.shape[2]
    row_loads = [
        pltpu.make_async_copy(
            meas.at[:, pl.ds(pl.multiple_of(g * rows_here + tile_row, tile_rows), tile_rows), :],
            rows_in.at[g],
            sems.at[ROWS_LOCAL],
        )
        for g in range(group_count)
    ]
    small_loads = [
        pltpu.make_async_copy(src, dst, small_sems.at[k])
        for k, (src, dst) in enumerate(((shift_in, shift), (frac_in, frac), (spec_in, spec), (att_in, att)))
    ]
    held_load = pltpu.make_async_copy(dens.at[pl.ds(group * rows_here, rows_here)], held, small_sems.at[4])
    for load in small_loads[:2]:
        load.start()

    barrier = pltpu.get_barrier_semaphore()

    def greet(to):
        pl.semaphore_signal(barrier, inc=1, device_id=to, device_id_type=MESH)

    def greet_depth(k, carry):
        greet(at(group, (depth + k) % depth_count, lat))
        return carry

    lax.fori_loop(1, depth_count, greet_depth, 0, unroll=True)
    for g in range(1, group_count):
        greet(at((group + g) % group_count, depth, lat))

    @pl.when(has_halo)
    def _():
        def greet_halo(k, carry):
            greet(at(group, (depth + k) % depth_count, halo_from))
            return carry

        lax.fori_loop(0, depth_count, greet_halo, 0, unroll=True)
        for g in range(1, group_count):
            greet(at((group + g) % group_count, depth, halo_from))

    for load in [held_load] + row_loads + small_loads[2:]:
        load.start()

    sub = lax.broadcasted_iota(jnp.int32, (depth_here, LANES), 0)
    lane4 = lax.broadcasted_iota(jnp.int32, (depth_here, LANES), 1)
    place = lane4 % 32 - group * views_here
    for load in small_loads[:2]:
        load.wait()
    shifts = jnp.zeros((depth_here, LANES), jnp.int32)
    fracs = jnp.zeros((depth_here, LANES), jnp.float32)
    for v in range(views_here):
        for z in range(depth_here):
            here = (sub == z) & (place == v)
            shifts = jnp.where(here, shift[v, z] + HALO, shifts)
            fracs = jnp.where(here, frac[v, z], fracs)
    mine = (place >= 0) & (place < views_here) & (lane4 < 96)
    weights = jnp.where(lane4 < 64, 1.0 - fracs, fracs).astype(jnp.bfloat16).astype(jnp.float32)
    shear_x[group] = jnp.where(mine, jnp.where(lane4 < 32, shifts.astype(jnp.float32), weights), 0.0)

    some = min(depth_count // 2, split)
    expected = (
        depth_count - 1 + group_count - 1
        + jnp.where(has_left, depth_count // 2, 0)
        + jnp.where(has_right, depth_count // 2, 0)
        + jnp.where(gives_halo, group_count - 1, 0)
    )
    held_load.wait()
    drain(rows_in, sems.at[ROWS_LOCAL])
    row = (depth // 2) % tile_rows
    for g in range(group_count):
        for v in range(views_here):
            rows_mine[g, v : v + 1, :] = rows_in[g, v, pl.ds(row, 1), :]
    pl.semaphore_wait(barrier, expected)

    for g in range(1, group_count):
        remote(
            shear_x.at[group], shear_x.at[group], sems.at[SHX_SEND], sems.at[SHX_RECV],
            at((group + g) % group_count, depth, lat),
        ).start()

    def own_part(depth_to):
        half_to = depth_to % 2
        src = held.at[depth_to // 2, :, :, lanes(half_to * LANES, 3 * LANES)]
        dst = slabs.at[depth, :, :, lanes((1 - half_to) * LANES, 3 * LANES)]
        return src, dst

    def send_halo(depth_to, batch):
        here = held.at[depth_to // 2]

        @pl.when((depth_to % 2 == 0) & has_right)
        def _():
            remote(
                here.at[:, :, 3 * LANES : 4 * LANES], slabs.at[depth, :, :, 0:LANES],
                sems.at[RIGHT_SEND], halo_recv.at[batch], at(group, depth_to, lat + 1),
            ).start()

        @pl.when((depth_to % 2 == 1) & has_left)
        def _():
            remote(
                here.at[:, :, 0:LANES], slabs.at[depth, :, :, 3 * LANES : 4 * LANES],
                sems.at[LEFT_SEND], halo_recv.at[batch], at(group, depth_to, lat - 1),
            ).start()

    def send_slab(batch, k, carry):
        depth_to = partner(k)
        src, dst = own_part(depth_to)
        remote(
            src, dst, sems.at[OWN_SEND], own_recv.at[batch], at(group, depth_to, lat)
        ).start()
        send_halo(depth_to, batch)
        return carry

    src, dst = own_part(depth)
    pltpu.make_async_copy(src, dst, own_recv.at[batches - 1]).start()
    lax.fori_loop(0, some, functools.partial(send_slab, 0), 0)

    drain(shear_x.at[0 : group_count - 1], sems.at[SHX_RECV])
    table = shear_x[0]
    for g in range(1, group_count):
        table = table + shear_x[g]
    shear_mine[...] = table
    shear_all[depth] = table

    def send_shear(k, carry):
        depth_to = partner(k)
        remote(
            shear_mine, shear_all.at[depth], sems.at[SH_SEND], sems.at[SH_RECV], at(group, depth_to, lat)
        ).start()
        return carry

    lax.fori_loop(0, depth_count - 1, send_shear, 0)
    lax.fori_loop(some, min(split, depth_count - 1), functools.partial(send_slab, 0), 0)
    lax.fori_loop(split, depth_count - 1, functools.partial(send_slab, batches - 1), 0)
    send_halo(depth, batches - 1)

    @pl.when(jnp.logical_not(has_halo) & (half == 0))
    def _():
        slabs[:, :, :, 0:LANES] = jnp.zeros((depth_count, materials, depth_here, LANES), jnp.bfloat16)

    @pl.when(jnp.logical_not(has_halo) & (half == 1))
    def _():
        slabs[:, :, :, 3 * LANES : 4 * LANES] = jnp.zeros(
            (depth_count, materials, depth_here, LANES), jnp.bfloat16
        )

    for k in range(group_count):
        g = (group + k) % group_count
        src = rows_mine.at[g, :, lanes(half * LANES, 3 * LANES)]
        dst = rows_all.at[group, :, lanes((1 - half) * LANES, 3 * LANES)]
        if k == 0:
            pltpu.make_async_copy(src, dst, sems.at[ROWS_RECV]).start()
        else:
            remote(src, dst, sems.at[ROWS_SEND], sems.at[ROWS_RECV], at(g, depth, lat)).start()

    @pl.when(gives_halo)
    def _():
        for k in range(group_count):
            g = (group + k) % group_count
            remote(
                rows_mine.at[g, :, lanes((1 - half) * (3 * LANES), LANES)],
                rows_all.at[group, :, lanes(half * (3 * LANES), LANES)],
                sems.at[EDGE_SEND], sems.at[EDGE_RECV], at(g, depth, halo_to),
            ).start()

    source = lax.broadcasted_iota(jnp.int32, (LANES, KINDS), 0)
    wanted = lax.broadcasted_iota(jnp.int32, (LANES, KINDS), 1) // LANES * 32
    for v in range(view_count):
        spread[v] = (source == wanted + v).astype(jnp.float32).astype(jnp.bfloat16)

    lane = lax.broadcasted_iota(jnp.int32, (8, LANES), 1)
    drain(shear_all.at[0 : depth_count - 1], sems.at[SH_RECV])
    table = jnp.concatenate([shear_all[p] for p in range(depth_count)], axis=0).astype(jnp.bfloat16)

    def widen(v, carry):
        wide = jnp.dot(table, spread[v], preferred_element_type=jnp.float32)
        for p in range(pair_count):
            rows = wide[8 * p : 8 * p + 8]
            shift_wide[v, p] = rows[:, 0:LANES].astype(jnp.int32)
            weight_wide[v, p, 0] = rows[:, LANES : 2 * LANES]
            weight_wide[v, p, 1] = rows[:, 2 * LANES : 3 * LANES]
        return carry

    lax.fori_loop(0, view_count, widen, 0, unroll=4)

    for batch, (step_from, step_to) in enumerate(parts_of):
        share = (step_to - step_from) * z_count
        drain(slabs.at[0:share, :, :, 0 : 3 * LANES], own_recv.at[batch])

        @pl.when(has_halo)
        def _():
            drain(slabs.at[0:share, :, :, 0:LANES], halo_recv.at[batch])

        pairs = []
        for step in range(step_from, step_to):
            y_step = far_first(step, y_count)
            y_from = lax.rem(y_here + jnp.where(lat % 2 == 1, y_step, y_count - y_step), y_count)
            pairs += [2 * y_from, 2 * y_from + 1]
        for p, pair in enumerate(pairs):
            for m in range(materials):
                first = slabs[2 * pair, m].astype(jnp.float32)
                second = slabs[2 * pair + 1, m].astype(jnp.float32)
                planes[p, m] = jnp.concatenate([first, second], axis=0)

        def one_view(v, carry):
            zero = jnp.zeros((8, LANES), jnp.float32)
            low = [[zero if batch == 0 else acc[v, m, k] for k in range(3)] for m in range(materials)]
            up = [[zero if batch == 0 else acc[v, m, 3 + k] for k in range(4)] for m in range(materials)]
            for p, pair in enumerate(pairs):
                moved = lane + shift_wide[v, pair]
                index = moved & (LANES - 1)
                inside = moved < LANES
                lower = weight_wide[v, pair, 0]
                upper = weight_wide[v, pair, 1]
                for m in range(materials):
                    parts = [
                        take_lanes(planes[p, m, :, k * LANES : (k + 1) * LANES], index) for k in range(4)
                    ]
                    for k in range(3):
                        tap = jnp.where(inside, parts[k], parts[k + 1])
                        low[m][k] = low[m][k] + lower * tap
                        up[m][k] = up[m][k] + upper * tap
                    up[m][3] = up[m][3] + upper * parts[3]
            for m in range(materials):
                for k in range(3):
                    acc[v, m, k] = low[m][k]
                for k in range(4):
                    acc[v, m, 3 + k] = up[m][k]
            return carry

        lax.fori_loop(0, view_count, one_view, 0, unroll=4)

    for v in range(view_count):
        for m in range(materials):
            for k in range(3):
                low_rows[m, v : v + 1, k * LANES : (k + 1) * LANES] = jnp.sum(
                    acc[v, m, k], axis=0, keepdims=True
                )
            for k in range(4):
                up_rows[m, v : v + 1, k * LANES : (k + 1) * LANES] = jnp.sum(
                    acc[v, m, 3 + k], axis=0, keepdims=True
                )
    depth_all = depth_here * depth_count
    paths = [
        (low_rows[m] + pltpu.roll(up_rows[m], 4 * LANES - 1, 1)[:, 0 : 3 * LANES]) * (1.0 / depth_all)
        for m in range(materials)
    ]

    drain(rows_all.at[:, :, 0 : 3 * LANES], sems.at[ROWS_RECV])

    @pl.when(has_halo)
    def _():
        drain(rows_all.at[:, :, 0:LANES], sems.at[EDGE_RECV])

    observed = jnp.concatenate([rows_all[g] for g in range(group_count)], axis=0)
    observed = pltpu.roll(observed, 4 * LANES - HALO, 1)[:, 0 : 3 * LANES]
    blank = jnp.zeros((view_count, 3 * LANES), jnp.float32)
    for load in small_loads[2:]:
        load.wait()

    def one_bin(e, carry):
        intensity, water, bone, total = carry
        counts = spec[e] * jnp.exp(-(att[0, e] * paths[0] + att[1, e] * paths[1]))
        return (
            intensity + counts, water + att[0, e] * counts, bone + att[1, e] * counts, total + spec[e]
        )

    intensity, water, bone, total = lax.fori_loop(
        0, bins, one_bin, (blank, blank, blank, jnp.float32(0.0)), unroll=4
    )
    residual = jnp.log(blank + total) - jnp.log(intensity) - observed
    factor = residual / intensity / view_count
    column = lax.broadcasted_iota(jnp.int32, (view_count, 3 * LANES), 1)
    column = column + (lat * 4 + half * 2) * LANES - HALO
    valid = (column >= 0) & (column < lat_count * 4 * LANES)
    for m, moment in enumerate((water, bone)):
        grads[m] = jnp.where(valid, (moment * factor).astype(jnp.bfloat16).astype(jnp.float32), 0.0)

    part = pl.ds(pl.multiple_of(half * (2 * LANES), LANES), 2 * LANES)

    def one_pair(t, carry):
        y_step = far_first(t // 2, y_count)
        y_to = lax.rem(y_here + jnp.where(lat % 2 == 1, y_count - y_step, y_step), y_count)
        pair = y_to * 2 + (depth % z_count // 2 + 1 + t) % 2
        zero = jnp.zeros((8, LANES), jnp.float32)
        sums = [(zero,) * 5 for m in range(materials)]
        for v in range(view_count):
            moved = lane + (LANES - 1) - shift_wide[v, pair]
            index = moved & (LANES - 1)
            inside = moved < LANES
            lower = weight_wide[v, pair, 0]
            upper = weight_wide[v, pair, 1]
            for m in range(materials):
                a0, a1, a2, b0, b1 = sums[m]
                parts = [
                    take_lanes(
                        jnp.broadcast_to(grads[m, v : v + 1, k * LANES : (k + 1) * LANES], (8, LANES)), index
                    )
                    for k in range(3)
                ]
                tap0 = jnp.where(inside, parts[0], parts[1])
                tap1 = jnp.where(inside, parts[1], parts[2])
                sums[m] = (
                    a0 + lower * tap0, a1 + lower * tap1, a2 + lower * parts[2],
                    b0 + upper * tap0, b1 + upper * tap1,
                )
        for m in range(materials):
            a0, a1, a2, b0, b1 = sums[m]
            ahead = pltpu.roll(jnp.concatenate([a0, a1, a2], axis=1), 3 * LANES - 1, 1)[:, 0 : 2 * LANES]
            result = encode(ahead + jnp.concatenate([b0, b1], axis=1))
            product[2 * pair, m] = result[0:depth_here]
            product[2 * pair + 1, m] = result[depth_here : 2 * depth_here]
        for side in range(2):
            depth_to = 2 * pair + side
            src, dst = product.at[depth_to], out.at[depth // 2, :, :, part]

            @pl.when(depth_to != depth)
            def _():
                remote(src, dst, sems.at[OUT_SEND], sems.at[OUT_RECV], at(group, depth_to, lat)).start()

            @pl.when(depth_to == depth)
            def _():
                pltpu.make_async_copy(src, dst, sems.at[OUT_RECV]).start()

        return carry

    lax.fori_loop(0, pair_count, one_pair, 0, unroll=2)

    others = depth_count - 1
    drain(shear_x.at[0 : group_count - 1], sems.at[SHX_SEND])
    drain(shear_all.at[0:others], sems.at[SH_SEND])
    drain(slabs.at[0:others, :, :, 0 : 3 * LANES], sems.at[OWN_SEND])
    drain(rows_all.at[0 : group_count - 1, :, 0 : 3 * LANES], sems.at[ROWS_SEND])

    @pl.when(has_right)
    def _():
        drain(slabs.at[0:pair_count, :, :, 0:LANES], sems.at[RIGHT_SEND])

    @pl.when(has_left)
    def _():
        drain(slabs.at[0:pair_count, :, :, 0:LANES], sems.at[LEFT_SEND])

    @pl.when(gives_halo)
    def _():
        drain(rows_all.at[:, :, 0:LANES], sems.at[EDGE_SEND])

    drain(product.at[0:others], sems.at[OUT_SEND])
    drain(out, sems.at[OUT_RECV])


def per_device(density, measured, shear_shift, shear_frac, spectrum, attenuation):
    sizes = tuple(lax.axis_size(name) for name in ("views", "depth", "lat"))
    group_count, depth_count, lat_count = sizes
    row_total, materials, depth_here, tile_width = density.shape
    views_here = shear_shift.shape[0]
    view_count = views_here * group_count
    rows_out = row_total // group_count
    pair_count = depth_count // 2
    tile_rows = min(8, rows_out)
    f32, bf16 = jnp.float32, jnp.bfloat16
    hbm = pl.BlockSpec(memory_space=pltpu.HBM)
    codes = pl.pallas_call(
        functools.partial(kernel, sizes),
        out_shape=jax.ShapeDtypeStruct((rows_out, materials, depth_here, tile_width), jnp.int16),
        in_specs=[hbm] * 6,
        out_specs=pl.BlockSpec(memory_space=pl.ANY),
        scratch_shapes=[
            pltpu.SMEM(shear_shift.shape, jnp.int32),
            pltpu.SMEM(shear_frac.shape, f32),
            pltpu.SMEM(spectrum.shape, f32),
            pltpu.SMEM(attenuation.shape, f32),
            pltpu.VMEM((rows_out, materials, depth_here, tile_width), bf16),
            pltpu.VMEM((depth_count, materials, depth_here, tile_width), bf16),
            pltpu.VMEM((pair_count, materials, 8, tile_width), f32),
            pltpu.VMEM((group_count, views_here, tile_rows, tile_width), f32),
            pltpu.VMEM((group_count, views_here, tile_width), f32),
            pltpu.VMEM((group_count, views_here, tile_width), f32),
            pltpu.VMEM((group_count, depth_here, LANES), f32),
            pltpu.VMEM((depth_here, LANES), f32),
            pltpu.VMEM((depth_count, depth_here, LANES), f32),
            pltpu.VMEM((view_count, LANES, KINDS), bf16),
            pltpu.VMEM((view_count, pair_count, 8, LANES), jnp.int32),
            pltpu.VMEM((view_count, pair_count, 2, 8, LANES), f32),
            pltpu.VMEM((view_count, materials, 7, 8, LANES), f32),
            pltpu.VMEM((materials, view_count, 3 * LANES), f32),
            pltpu.VMEM((materials, view_count, 4 * LANES), f32),
            pltpu.VMEM((materials, view_count, 3 * LANES), f32),
            pltpu.VMEM((depth_count, materials, depth_here, 2 * LANES), jnp.int16),
            pltpu.SemaphoreType.DMA((14,)),
            pltpu.SemaphoreType.DMA((2,)),
            pltpu.SemaphoreType.DMA((2,)),
            pltpu.SemaphoreType.DMA((5,)),
        ],
        compiler_params=pltpu.CompilerParams(
            collective_id=0, has_side_effects=True, vmem_limit_bytes=60 * 2**20
        ),
        cost_estimate=pl.CostEstimate(
            flops=16 * 2**20, bytes_accessed=2 * 2**20, transcendentals=2**19
        ),
    )(density, measured, shear_shift, shear_frac, spectrum, attenuation)
    return decode(codes)


def solution(mesh):
    in_specs = (
        P(None, None, "depth", "lat"),
        P("views", None, "lat"),
        P("views", "depth"),
        P("views", "depth"),
        P(),
        P(),
    )
    out_specs = P("views", None, "depth", "lat")
    return jax.shard_map(
        per_device, mesh=mesh, in_specs=in_specs, out_specs=out_specs, check_vma=False
    )
```

```python
import functools
import math

import jax
import jax.numpy as jnp
from jax import lax
from jax.experimental import pallas as pl
from jax.experimental.pallas import tpu as pltpu
from jax.sharding import PartitionSpec as P

HALO = 64
LANES = 128
MESH = pl.DeviceIdType.MESH
FLOOR = 2.0**-17
STEPS = 32767.0 / math.log(1.0 + 256.0 / FLOOR)
KINDS = 3 * LANES
(SHX_SEND, SHX_RECV, SH_SEND, SH_RECV, OWN_SEND, LEFT_SEND, RIGHT_SEND, ROWS_LOCAL, ROWS_SEND,
 ROWS_RECV, EDGE_SEND, EDGE_RECV, OUT_SEND, OUT_RECV) = range(14)


def take_lanes(x, index):
    return jnp.take_along_axis(x, index, axis=1, mode="promise_in_bounds")


def encode(x):
    size = jnp.log(1.0 + jnp.abs(x) * (1.0 / FLOOR)) * STEPS
    return jnp.round(jnp.where(x < 0.0, -size, size)).astype(jnp.int32).astype(jnp.int16)


def decode(code):
    code = code.astype(jnp.float32)
    size = (jnp.exp(jnp.abs(code) * (1.0 / STEPS)) - 1.0) * FLOOR
    return jnp.where(code < 0.0, -size, size)


def kernel(
    sizes, dens, meas, shift_in, frac_in, spec_in, att_in, out, shift, frac, spec, att, held, slabs, planes, rows_in, rows_mine, rows_all,
    shear_x, shear_mine, shear_all, spread, shift_wide, weight_wide, acc, low_rows, up_rows,
    grads, product, sems, own_recv, halo_recv, small_sems,
):
    group_count, depth_count, lat_count = sizes
    views_here, depth_here, materials = shift.shape[0], shift.shape[1], dens.shape[1]
    rows_here = depth_count // 2
    view_count = group_count * views_here
    pair_count = depth_count // 2
    z_count = 4
    y_count = depth_count // z_count
    first_part = 1 + 2 * (y_count // 4) if y_count % 2 == 0 else y_count
    parts_of = [(0, first_part), (first_part, y_count)] if first_part < y_count else [(0, y_count)]
    batches = len(parts_of)
    split = first_part * z_count
    bins = spec.shape[0]
    group = lax.axis_index("views")
    depth = lax.axis_index("depth")
    lat = lax.axis_index("lat")
    half = depth % 2
    y_here, z_here = lax.div(depth, z_count), lax.rem(depth, z_count)
    has_left = lat > 0
    has_right = lat < lat_count - 1
    halo_from = jnp.where(half == 0, lat - 1, lat + 1)
    has_halo = jnp.where(half == 0, lat, lat_count - 1 - lat) > 0
    halo_to = jnp.where(half == 0, lat + 1, lat - 1)
    gives_halo = jnp.where(half == 0, lat_count - 1 - lat, lat) > 0

    def at(group_to, depth_to, lat_to):
        return {"views": group_to, "depth": depth_to, "lat": lat_to}

    def remote(src, dst, send, recv, to):
        return pltpu.make_async_remote_copy(
            src_ref=src, dst_ref=dst, send_sem=send, recv_sem=recv, device_id=to, device_id_type=MESH
        )

    def far_first(step, count):
        if isinstance(step, int):
            return count // 2 + (-((step + 1) // 2) if step % 2 else step // 2)
        return count // 2 + jnp.where(step % 2 == 1, -((step + 1) // 2), step // 2)

    def partner(step):
        y_step = far_first(step // z_count, y_count)
        z_step = far_first(step % z_count, z_count)
        y_to = lax.rem(y_here + jnp.where(lat % 2 == 1, y_count - y_step, y_step), y_count)
        z_to = lax.rem(z_here + jnp.where(lat % 2 == 1, z_count - z_step, z_step), z_count)
        return y_to * z_count + z_to

    def drain(ref, sem):
        pltpu.make_async_copy(ref, ref, sem).wait()

    def lanes(start, width):
        return pl.ds(pl.multiple_of(start, LANES), width)

    tile_row = pl.multiple_of((depth // 2) // 8 * 8, 8) if rows_here >= 8 else 0
    tile_rows = rows_in.shape[2]
    row_loads = [
        pltpu.make_async_copy(
            meas.at[:, pl.ds(pl.multiple_of(g * rows_here + tile_row, tile_rows), tile_rows), :],
            rows_in.at[g],
            sems.at[ROWS_LOCAL],
        )
        for g in range(group_count)
    ]
    small_loads = [
        pltpu.make_async_copy(src, dst, small_sems.at[k])
        for k, (src, dst) in enumerate(((shift_in, shift), (frac_in, frac), (spec_in, spec), (att_in, att)))
    ]
    held_load = pltpu.make_async_copy(dens.at[pl.ds(group * rows_here, rows_here)], held, small_sems.at[4])
    for load in small_loads[:2]:
        load.start()

    barrier = pltpu.get_barrier_semaphore()

    def greet(to):
        pl.semaphore_signal(barrier, inc=1, device_id=to, device_id_type=MESH)

    def greet_depth(k, carry):
        greet(at(group, (depth + k) % depth_count, lat))
        return carry

    lax.fori_loop(1, depth_count, greet_depth, 0, unroll=True)
    for g in range(1, group_count):
        greet(at((group + g) % group_count, depth, lat))

    @pl.when(has_halo)
    def _():
        def greet_halo(k, carry):
            greet(at(group, (depth + k) % depth_count, halo_from))
            return carry

        lax.fori_loop(0, depth_count, greet_halo, 0, unroll=True)
        for g in range(1, group_count):
            greet(at((group + g) % group_count, depth, halo_from))

    for load in [held_load] + row_loads + small_loads[2:]:
        load.start()

    sub = lax.broadcasted_iota(jnp.int32, (depth_here, LANES), 0)
    lane4 = lax.broadcasted_iota(jnp.int32, (depth_here, LANES), 1)
    place = lane4 % 32 - group * views_here
    for load in small_loads[:2]:
        load.wait()
    shifts = jnp.zeros((depth_here, LANES), jnp.int32)
    fracs = jnp.zeros((depth_here, LANES), jnp.float32)
    for v in range(views_here):
        for z in range(depth_here):
            here = (sub == z) & (place == v)
            shifts = jnp.where(here, shift[v, z] + HALO, shifts)
            fracs = jnp.where(here, frac[v, z], fracs)
    mine = (place >= 0) & (place < views_here) & (lane4 < 96)
    weights = jnp.where(lane4 < 64, 1.0 - fracs, fracs).astype(jnp.bfloat16).astype(jnp.float32)
    shear_x[group] = jnp.where(mine, jnp.where(lane4 < 32, shifts.astype(jnp.float32), weights), 0.0)

    some = min(depth_count // 2, split)
    expected = (
        depth_count - 1 + group_count - 1
        + jnp.where(has_left, depth_count // 2, 0)
        + jnp.where(has_right, depth_count // 2, 0)
        + jnp.where(gives_halo, group_count - 1, 0)
    )
    held_load.wait()
    drain(rows_in, sems.at[ROWS_LOCAL])
    row = (depth // 2) % tile_rows
    for g in range(group_count):
        for v in range(views_here):
            rows_mine[g, v : v + 1, :] = rows_in[g, v, pl.ds(row, 1), :]
    pl.semaphore_wait(barrier, expected)

    for g in range(1, group_count):
        remote(
            shear_x.at[group], shear_x.at[group], sems.at[SHX_SEND], sems.at[SHX_RECV],
            at((group + g) % group_count, depth, lat),
        ).start()

    def own_part(depth_to):
        half_to = depth_to % 2
        src = held.at[depth_to // 2, :, :, lanes(half_to * LANES, 3 * LANES)]
        dst = slabs.at[depth, :, :, lanes((1 - half_to) * LANES, 3 * LANES)]
        return src, dst

    def send_halo(depth_to, batch):
        here = held.at[depth_to // 2]

        @pl.when((depth_to % 2 == 0) & has_right)
        def _():
            remote(
                here.at[:, :, 3 * LANES : 4 * LANES], slabs.at[depth, :, :, 0:LANES],
                sems.at[RIGHT_SEND], halo_recv.at[batch], at(group, depth_to, lat + 1),
            ).start()

        @pl.when((depth_to % 2 == 1) & has_left)
        def _():
            remote(
                here.at[:, :, 0:LANES], slabs.at[depth, :, :, 3 * LANES : 4 * LANES],
                sems.at[LEFT_SEND], halo_recv.at[batch], at(group, depth_to, lat - 1),
            ).start()

    def send_slab(batch, k, carry):
        depth_to = partner(k)
        src, dst = own_part(depth_to)
        remote(
            src, dst, sems.at[OWN_SEND], own_recv.at[batch], at(group, depth_to, lat)
        ).start()
        send_halo(depth_to, batch)
        return carry

    src, dst = own_part(depth)
    pltpu.make_async_copy(src, dst, own_recv.at[batches - 1]).start()
    lax.fori_loop(0, some, functools.partial(send_slab, 0), 0)

    drain(shear_x.at[0 : group_count - 1], sems.at[SHX_RECV])
    table = shear_x[0]
    for g in range(1, group_count):
        table = table + shear_x[g]
    shear_mine[...] = table
    shear_all[depth] = table

    def send_shear(k, carry):
        depth_to = partner(k)
        remote(
            shear_mine, shear_all.at[depth], sems.at[SH_SEND], sems.at[SH_RECV], at(group, depth_to, lat)
        ).start()
        return carry

    lax.fori_loop(0, depth_count - 1, send_shear, 0)
    lax.fori_loop(some, min(split, depth_count - 1), functools.partial(send_slab, 0), 0)
    lax.fori_loop(split, depth_count - 1, functools.partial(send_slab, batches - 1), 0)
    send_halo(depth, batches - 1)

    @pl.when(jnp.logical_not(has_halo) & (half == 0))
    def _():
        slabs[:, :, :, 0:LANES] = jnp.zeros((depth_count, materials, depth_here, LANES), jnp.bfloat16)

    @pl.when(jnp.logical_not(has_halo) & (half == 1))
    def _():
        slabs[:, :, :, 3 * LANES : 4 * LANES] = jnp.zeros(
            (depth_count, materials, depth_here, LANES), jnp.bfloat16
        )

    for k in range(group_count):
        g = (group + k) % group_count
        src = rows_mine.at[g, :, lanes(half * LANES, 3 * LANES)]
        dst = rows_all.at[group, :, lanes((1 - half) * LANES, 3 * LANES)]
        if k == 0:
            pltpu.make_async_copy(src, dst, sems.at[ROWS_RECV]).start()
        else:
            remote(src, dst, sems.at[ROWS_SEND], sems.at[ROWS_RECV], at(g, depth, lat)).start()

    @pl.when(gives_halo)
    def _():
        for k in range(group_count):
            g = (group + k) % group_count
            remote(
                rows_mine.at[g, :, lanes((1 - half) * (3 * LANES), LANES)],
                rows_all.at[group, :, lanes(half * (3 * LANES), LANES)],
                sems.at[EDGE_SEND], sems.at[EDGE_RECV], at(g, depth, halo_to),
            ).start()

    source = lax.broadcasted_iota(jnp.int32, (LANES, KINDS), 0)
    wanted = lax.broadcasted_iota(jnp.int32, (LANES, KINDS), 1) // LANES * 32
    for v in range(view_count):
        spread[v] = (source == wanted + v).astype(jnp.float32).astype(jnp.bfloat16)

    lane = lax.broadcasted_iota(jnp.int32, (8, LANES), 1)
    drain(shear_all.at[0 : depth_count - 1], sems.at[SH_RECV])
    table = jnp.concatenate([shear_all[p] for p in range(depth_count)], axis=0).astype(jnp.bfloat16)

    def widen(v, carry):
        wide = jnp.dot(table, spread[v], preferred_element_type=jnp.float32)
        for p in range(pair_count):
            rows = wide[8 * p : 8 * p + 8]
            shift_wide[v, p] = rows[:, 0:LANES].astype(jnp.int32)
            weight_wide[v, p, 0] = rows[:, LANES : 2 * LANES]
            weight_wide[v, p, 1] = rows[:, 2 * LANES : 3 * LANES]
        return carry

    lax.fori_loop(0, view_count, widen, 0, unroll=4)

    for batch, (step_from, step_to) in enumerate(parts_of):
        share = (step_to - step_from) * z_count
        drain(slabs.at[0:share, :, :, 0 : 3 * LANES], own_recv.at[batch])

        @pl.when(has_halo)
        def _():
            drain(slabs.at[0:share, :, :, 0:LANES], halo_recv.at[batch])

        pairs = []
        for step in range(step_from, step_to):
            y_step = far_first(step, y_count)
            y_from = lax.rem(y_here + jnp.where(lat % 2 == 1, y_step, y_count - y_step), y_count)
            pairs += [2 * y_from, 2 * y_from + 1]
        for p, pair in enumerate(pairs):
            for m in range(materials):
                first = slabs[2 * pair, m].astype(jnp.float32)
                second = slabs[2 * pair + 1, m].astype(jnp.float32)
                planes[p, m] = jnp.concatenate([first, second], axis=0)

        def one_view(v, carry):
            zero = jnp.zeros((8, LANES), jnp.float32)
            low = [[zero if batch == 0 else acc[v, m, k] for k in range(3)] for m in range(materials)]
            up = [[zero if batch == 0 else acc[v, m, 3 + k] for k in range(4)] for m in range(materials)]
            for p, pair in enumerate(pairs):
                moved = lane + shift_wide[v, pair]
                index = moved & (LANES - 1)
                inside = moved < LANES
                lower = weight_wide[v, pair, 0]
                upper = weight_wide[v, pair, 1]
                for m in range(materials):
                    parts = [
                        take_lanes(planes[p, m, :, k * LANES : (k + 1) * LANES], index) for k in range(4)
                    ]
                    for k in range(3):
                        tap = jnp.where(inside, parts[k], parts[k + 1])
                        low[m][k] = low[m][k] + lower * tap
                        up[m][k] = up[m][k] + upper * tap
                    up[m][3] = up[m][3] + upper * parts[3]
            for m in range(materials):
                for k in range(3):
                    acc[v, m, k] = low[m][k]
                for k in range(4):
                    acc[v, m, 3 + k] = up[m][k]
            return carry

        lax.fori_loop(0, view_count, one_view, 0, unroll=8)

    for v in range(view_count):
        for m in range(materials):
            for k in range(3):
                low_rows[m, v : v + 1, k * LANES : (k + 1) * LANES] = jnp.sum(
                    acc[v, m, k], axis=0, keepdims=True
                )
            for k in range(4):
                up_rows[m, v : v + 1, k * LANES : (k + 1) * LANES] = jnp.sum(
                    acc[v, m, 3 + k], axis=0, keepdims=True
                )
    depth_all = depth_here * depth_count
    paths = [
        (low_rows[m] + pltpu.roll(up_rows[m], 4 * LANES - 1, 1)[:, 0 : 3 * LANES]) * (1.0 / depth_all)
        for m in range(materials)
    ]

    drain(rows_all.at[:, :, 0 : 3 * LANES], sems.at[ROWS_RECV])

    @pl.when(has_halo)
    def _():
        drain(rows_all.at[:, :, 0:LANES], sems.at[EDGE_RECV])

    observed = jnp.concatenate([rows_all[g] for g in range(group_count)], axis=0)
    observed = pltpu.roll(observed, 4 * LANES - HALO, 1)[:, 0 : 3 * LANES]
    blank = jnp.zeros((view_count, 3 * LANES), jnp.float32)
    for load in small_loads[2:]:
        load.wait()

    def one_bin(e, carry):
        intensity, water, bone, total = carry
        counts = spec[e] * jnp.exp(-(att[0, e] * paths[0] + att[1, e] * paths[1]))
        return (
            intensity + counts, water + att[0, e] * counts, bone + att[1, e] * counts, total + spec[e]
        )

    intensity, water, bone, total = lax.fori_loop(
        0, bins, one_bin, (blank, blank, blank, jnp.float32(0.0)), unroll=4
    )
    residual = jnp.log(blank + total) - jnp.log(intensity) - observed
    factor = residual / intensity / view_count
    column = lax.broadcasted_iota(jnp.int32, (view_count, 3 * LANES), 1)
    column = column + (lat * 4 + half * 2) * LANES - HALO
    valid = (column >= 0) & (column < lat_count * 4 * LANES)
    for m, moment in enumerate((water, bone)):
        grads[m] = jnp.where(valid, (moment * factor).astype(jnp.bfloat16).astype(jnp.float32), 0.0)

    part = pl.ds(pl.multiple_of(half * (2 * LANES), LANES), 2 * LANES)

    def one_pair(t, carry):
        y_step = far_first(t // 2, y_count)
        y_to = lax.rem(y_here + jnp.where(lat % 2 == 1, y_count - y_step, y_step), y_count)
        pair = y_to * 2 + (depth % z_count // 2 + 1 + t) % 2
        zero = jnp.zeros((8, LANES), jnp.float32)
        sums = [(zero,) * 5 for m in range(materials)]
        for v in range(view_count):
            moved = lane + (LANES - 1) - shift_wide[v, pair]
            index = moved & (LANES - 1)
            inside = moved < LANES
            lower = weight_wide[v, pair, 0]
            upper = weight_wide[v, pair, 1]
            for m in range(materials):
                a0, a1, a2, b0, b1 = sums[m]
                parts = [
                    take_lanes(
                        jnp.broadcast_to(grads[m, v : v + 1, k * LANES : (k + 1) * LANES], (8, LANES)), index
                    )
                    for k in range(3)
                ]
                tap0 = jnp.where(inside, parts[0], parts[1])
                tap1 = jnp.where(inside, parts[1], parts[2])
                sums[m] = (
                    a0 + lower * tap0, a1 + lower * tap1, a2 + lower * parts[2],
                    b0 + upper * tap0, b1 + upper * tap1,
                )
        for m in range(materials):
            a0, a1, a2, b0, b1 = sums[m]
            ahead = pltpu.roll(jnp.concatenate([a0, a1, a2], axis=1), 3 * LANES - 1, 1)[:, 0 : 2 * LANES]
            result = encode(ahead + jnp.concatenate([b0, b1], axis=1))
            product[2 * pair, m] = result[0:depth_here]
            product[2 * pair + 1, m] = result[depth_here : 2 * depth_here]
        for side in range(2):
            depth_to = 2 * pair + side
            src, dst = product.at[depth_to], out.at[depth // 2, :, :, part]

            @pl.when(depth_to != depth)
            def _():
                remote(src, dst, sems.at[OUT_SEND], sems.at[OUT_RECV], at(group, depth_to, lat)).start()

            @pl.when(depth_to == depth)
            def _():
                pltpu.make_async_copy(src, dst, sems.at[OUT_RECV]).start()

        return carry

    lax.fori_loop(0, pair_count, one_pair, 0, unroll=4)

    others = depth_count - 1
    drain(shear_x.at[0 : group_count - 1], sems.at[SHX_SEND])
    drain(shear_all.at[0:others], sems.at[SH_SEND])
    drain(slabs.at[0:others, :, :, 0 : 3 * LANES], sems.at[OWN_SEND])
    drain(rows_all.at[0 : group_count - 1, :, 0 : 3 * LANES], sems.at[ROWS_SEND])

    @pl.when(has_right)
    def _():
        drain(slabs.at[0:pair_count, :, :, 0:LANES], sems.at[RIGHT_SEND])

    @pl.when(has_left)
    def _():
        drain(slabs.at[0:pair_count, :, :, 0:LANES], sems.at[LEFT_SEND])

    @pl.when(gives_halo)
    def _():
        drain(rows_all.at[:, :, 0:LANES], sems.at[EDGE_SEND])

    drain(product.at[0:others], sems.at[OUT_SEND])
    drain(out, sems.at[OUT_RECV])


def per_device(density, measured, shear_shift, shear_frac, spectrum, attenuation):
    sizes = tuple(lax.axis_size(name) for name in ("views", "depth", "lat"))
    group_count, depth_count, lat_count = sizes
    row_total, materials, depth_here, tile_width = density.shape
    views_here = shear_shift.shape[0]
    view_count = views_here * group_count
    rows_out = row_total // group_count
    pair_count = depth_count // 2
    tile_rows = min(8, rows_out)
    f32, bf16 = jnp.float32, jnp.bfloat16
    hbm = pl.BlockSpec(memory_space=pltpu.HBM)
    codes = pl.pallas_call(
        functools.partial(kernel, sizes),
        out_shape=jax.ShapeDtypeStruct((rows_out, materials, depth_here, tile_width), jnp.int16),
        in_specs=[hbm] * 6,
        out_specs=pl.BlockSpec(memory_space=pl.ANY),
        scratch_shapes=[
            pltpu.SMEM(shear_shift.shape, jnp.int32),
            pltpu.SMEM(shear_frac.shape, f32),
            pltpu.SMEM(spectrum.shape, f32),
            pltpu.SMEM(attenuation.shape, f32),
            pltpu.VMEM((rows_out, materials, depth_here, tile_width), bf16),
            pltpu.VMEM((depth_count, materials, depth_here, tile_width), bf16),
            pltpu.VMEM((pair_count, materials, 8, tile_width), f32),
            pltpu.VMEM((group_count, views_here, tile_rows, tile_width), f32),
            pltpu.VMEM((group_count, views_here, tile_width), f32),
            pltpu.VMEM((group_count, views_here, tile_width), f32),
            pltpu.VMEM((group_count, depth_here, LANES), f32),
            pltpu.VMEM((depth_here, LANES), f32),
            pltpu.VMEM((depth_count, depth_here, LANES), f32),
            pltpu.VMEM((view_count, LANES, KINDS), bf16),
            pltpu.VMEM((view_count, pair_count, 8, LANES), jnp.int32),
            pltpu.VMEM((view_count, pair_count, 2, 8, LANES), f32),
            pltpu.VMEM((view_count, materials, 7, 8, LANES), f32),
            pltpu.VMEM((materials, view_count, 3 * LANES), f32),
            pltpu.VMEM((materials, view_count, 4 * LANES), f32),
            pltpu.VMEM((materials, view_count, 3 * LANES), f32),
            pltpu.VMEM((depth_count, materials, depth_here, 2 * LANES), jnp.int16),
            pltpu.SemaphoreType.DMA((14,)),
            pltpu.SemaphoreType.DMA((2,)),
            pltpu.SemaphoreType.DMA((2,)),
            pltpu.SemaphoreType.DMA((5,)),
        ],
        compiler_params=pltpu.CompilerParams(
            collective_id=0, has_side_effects=True, vmem_limit_bytes=60 * 2**20
        ),
        cost_estimate=pl.CostEstimate(
            flops=16 * 2**20, bytes_accessed=2 * 2**20, transcendentals=2**19
        ),
    )(density, measured, shear_shift, shear_frac, spectrum, attenuation)
    return decode(codes)


def solution(mesh):
    in_specs = (
        P(None, None, "depth", "lat"),
        P("views", None, "lat"),
        P("views", "depth"),
        P("views", "depth"),
        P(),
        P(),
    )
    out_specs = P("views", None, "depth", "lat")
    return jax.shard_map(
        per_device, mesh=mesh, in_specs=in_specs, out_specs=out_specs, check_vma=False
    )
```
